512 devices in a mesh: lat: 16 (over z_lo, core), lon: 32 (over x, z_hi, y).
Axes of the slice: x: 4, y: 4, z: 16 (z_hi: 2, z_lo: 8; z = z_hi * 8 + z_lo), core: 2. Of those that a mesh axis runs over, the one named last changes fastest.
Arguments:
- tokens: bfloat16 [192, 768, 512], P('lat', 'lon'), may hold values from -6 to 6
- fine_qkv: bfloat16 [512, 1536], P('lat'), may hold values from -0.25 to 0.25
- fine_out: bfloat16 [512, 512], P('lat'), may hold values from -0.25 to 0.25
- fine_scale: float32 [8], replicated, may hold values from 2 to 16
- fine_table: float32 [253, 8], replicated, may hold values from -3 to 3
- fine_gain: float32 [512], replicated, may hold values from 0.5 to 1.5
- merge_weight: bfloat16 [2048, 512], P('lat'), may hold values from -0.125 to 0.125
- merge_gain: float32 [512], replicated, may hold values from 0.5 to 1.5
- coarse_qkv: bfloat16 [512, 1536], P('lat'), may hold values from -0.25 to 0.25
- coarse_out: bfloat16 [512, 512], P('lat'), may hold values from -0.25 to 0.25
- coarse_scale: float32 [8], replicated, may hold values from 2 to 16
- coarse_table: float32 [253, 8], replicated, may hold values from -3 to 3
- coarse_gain: float32 [512], replicated, may hold values from 0.5 to 1.5
- shifts: int32 [2, 2], replicated, may hold values from 1 to 11, as said below
- bias_index: int32 [72, 72], replicated, may hold values from 0 to 252
Outputs:
- refined: bfloat16 [192, 768, 512], P('lat', 'lon')
The draws below stay inside these ranges and needn't reach their ends.
Inputs may be any that keep to these rules, and one draw needn't show every extreme that they name: `shifts`: row 0 serves the fine level and row 1 the coarse one; the first entry of a row lies in 1 to 5, the second in 1 to 11; one level's row shift is 1 and one level's column shift is 11.
All inputs are finite; a program needn't handle non-finite values.
Results may differ from the reference program's by a relative error of at most 0.017.
Values may be sent and summed in bfloat16 or wider, within the bound.
A program may use at most 64 MiB of HBM per device.

```python
import math
import jax
import jax.numpy as jnp
from jax import lax

D = 512
D2 = 512
HEADS = 8
HEADS2 = 8
WLAT = 6
WLON = 12
RELS = 253
WIN = 72
LAT = 192
LON = 768


def paired(key, fixed, upper):
    other_key, flip_key = jax.random.split(key)
    other = jax.random.randint(other_key, (), 1, upper, dtype=jnp.int32)
    flip = jax.random.randint(flip_key, (), 0, 2, dtype=jnp.int32)
    fixed_value = jnp.asarray(fixed, dtype=jnp.int32)
    first = jnp.where(flip == 0, fixed_value, other)
    second = jnp.where(flip == 0, other, fixed_value)
    return jnp.stack([first, second]).reshape(2, 1)


def draw_shifts(key, part):
    key = jax.random.fold_in(key, 7)
    lat_key, lon_key = jax.random.split(key)
    lat_shift = paired(lat_key, 1, WLAT)
    lon_shift = paired(lon_key, WLON - 1, WLON)
    return jnp.concatenate([lat_shift, lon_shift], axis=1)


def touch_ends(array, key, low, high):
    extent = array.shape
    place = [jax.random.randint(jax.random.fold_in(key, axis), (), 0, extent[axis]) for axis in range(len(extent))]
    array = array.at[tuple(place)].set(low)
    longest = extent.index(max(extent))
    place[longest] = (place[longest] + 1) % extent[longest]
    return array.at[tuple(place)].set(high)


def block_scale(own_key, shape, pieces, smallest, high):
    level = 1.0
    for axis_at, blocks in pieces:
        heights = jax.random.uniform(jax.random.fold_in(jax.random.fold_in(own_key, 6), axis_at), (blocks,), jnp.float32, smallest / len(pieces), high / len(pieces))
        level = level * jnp.repeat(jnp.exp(heights), shape[axis_at] // blocks).reshape((-1,) + (1,) * (len(shape) - 1 - axis_at))
    return level


def noise(rng, extent, deviation, most, pieces=(), held_as=jnp.bfloat16):
    array = jax.random.normal(rng, extent, jnp.float32) * deviation
    if len(pieces) > 0:
        array = block_scale(rng, extent, pieces, -0.22, 0.18) * array
    return jnp.clip(array, min=-most, max=most).astype(held_as)


def setup_inputs(seed: int = 0) -> dict:
    seeds = jax.random.split(jax.random.key(seed), 16)
    return {
        "tokens": noise(seeds[0], (LAT, LON, D), 1.0, 6.0, ((0, 16), (1, 32))),
        "fine_qkv": noise(seeds[1], (D, 3 * D), D ** -0.5, 0.25, ((0, 16),)),
        "fine_out": noise(seeds[2], (D, D), D ** -0.5, 0.25, ((0, 16),)),
        "fine_scale": jnp.clip(jnp.exp(jax.random.uniform(seeds[3], (HEADS,), jnp.float32, math.log(2.0), math.log(16.0))), 2.0, 16.0),
        "fine_table": noise(seeds[4], (RELS, HEADS), 1.0, 3.0, (), jnp.float32),
        "fine_gain": jnp.clip(1.0 + 0.1 * jax.random.normal(seeds[5], (D,), jnp.float32), 0.5, 1.5),
        "merge_weight": noise(seeds[6], (4 * D, D2), (4 * D) ** -0.5, 0.125, ((0, 16),)),
        "merge_gain": jnp.clip(1.0 + 0.1 * jax.random.normal(seeds[7], (D2,), jnp.float32), 0.5, 1.5),
        "coarse_qkv": noise(seeds[8], (D2, 3 * D2), D2 ** -0.5, 0.25, ((0, 16),)),
        "coarse_out": noise(seeds[9], (D2, D2), D2 ** -0.5, 0.25, ((0, 16),)),
        "coarse_scale": jnp.clip(jnp.exp(jax.random.uniform(seeds[10], (HEADS2,), jnp.float32, math.log(2.0), math.log(16.0))), 2.0, 16.0),
        "coarse_table": noise(seeds[11], (RELS, HEADS2), 1.0, 3.0, (), jnp.float32),
        "coarse_gain": jnp.clip(1.0 + 0.1 * jax.random.normal(seeds[12], (D2,), jnp.float32), 0.5, 1.5),
        "shifts": draw_shifts(jax.random.fold_in(seeds[15], 71), 0),
        "bias_index": touch_ends(jax.random.randint(seeds[14], (WIN, WIN), 0, RELS), jax.random.fold_in(seeds[14], 1), 0, RELS - 1).astype(jnp.int32),
    }


def layer_norm(values, gain):
    middle = lax.optimization_barrier(jnp.mean(values, axis=-1, keepdims=True))
    centered = values - middle
    spread = lax.optimization_barrier(jnp.mean(centered * centered, axis=-1, keepdims=True))
    return centered * lax.rsqrt(spread + 1e-05) * gain

def attend(query, keyval, keep, scale, bias, heads):
    number, window, width = query.shape
    depth = width // heads
    query_full = query.reshape(number, window, heads, depth).astype(jnp.float32)
    key_full = keyval[:, :, :width].reshape(number, window, heads, depth).astype(jnp.float32)
    value_full = keyval[:, :, width:].reshape(number, window, heads, depth).astype(jnp.float32)
    query_unit = query_full * lax.rsqrt(lax.optimization_barrier(jnp.sum(query_full * query_full, axis=-1, keepdims=True)) + 1e-06)
    key_unit = key_full * lax.rsqrt(lax.optimization_barrier(jnp.sum(key_full * key_full, axis=-1, keepdims=True)) + 1e-06)
    cosine = jnp.einsum('nqhd,nkhd->nhqk', query_unit, key_unit, precision=lax.Precision.HIGHEST)
    scores = scale[None, :, None, None] * cosine + bias[None]
    powers = jnp.exp(scores) * keep[:, None, None, :]
    weights = (powers / lax.optimization_barrier(jnp.sum(powers, axis=-1, keepdims=True))).astype(jnp.bfloat16)
    mixed = jnp.einsum('nhqk,nkhd->nqhd', weights.astype(jnp.float32), value_full)
    return mixed.reshape(number, window, width).astype(jnp.bfloat16)

def sublayer(grid, w_qkv, w_out, scale, table, gain, shift, bias_index, heads):
    rows, columns, width = grid.shape
    shift_lat = shift[0]
    shift_lon = shift[1]
    rolled = jnp.roll(grid, -shift_lon, axis=1)
    blank = jnp.zeros((WLAT, columns, width), grid.dtype)
    padded = jnp.concatenate([blank, rolled, blank], axis=0)
    span = rows + WLAT
    framed = lax.dynamic_slice_in_dim(padded, shift_lat, span, 0)
    latitude = jnp.arange(span, dtype=jnp.int32) + shift_lat - WLAT
    present = ((latitude >= 0) & (latitude < rows)).astype(jnp.float32)
    bias = table[bias_index].transpose(2, 0, 1)
    blocks = framed.reshape(span // WLAT, WLAT, columns, width)
    presence = present.reshape(span // WLAT, WLAT)
    per_row = columns // WLON

    def one_row(pair):
        block, alive = pair
        wins = block.reshape(WLAT, per_row, WLON, width).transpose(1, 0, 2, 3).reshape(per_row, WLAT * WLON, width)
        keep_one = jnp.broadcast_to(alive[:, None], (WLAT, WLON)).reshape(1, WLAT * WLON)
        keep = jnp.broadcast_to(keep_one, (per_row, WLAT * WLON))
        flat = wins.reshape(-1, width)
        projected = jnp.dot(flat, w_qkv, preferred_element_type=jnp.float32).astype(jnp.bfloat16)
        projected = projected.reshape(per_row, WLAT * WLON, 3 * width)
        mixed = attend(projected[:, :, :width], projected[:, :, width:], keep, scale, bias, heads)
        branch = jnp.dot(mixed.reshape(-1, width), w_out, preferred_element_type=jnp.float32)
        result = (flat.astype(jnp.float32) + layer_norm(branch, gain)).astype(jnp.bfloat16)
        return result.reshape(per_row, WLAT, WLON, width).transpose(1, 0, 2, 3).reshape(WLAT, columns, width)
    done = lax.map(one_row, (blocks, presence)).reshape(span, columns, width)
    own = lax.dynamic_slice_in_dim(done, WLAT - shift_lat, rows, 0)
    return jnp.roll(own, shift_lon, axis=1)

def reference(tokens, fine_qkv, fine_out, fine_scale, fine_table, fine_gain, merge_weight, merge_gain, coarse_qkv, coarse_out, coarse_scale, coarse_table, coarse_gain, shifts, bias_index):
    fine_after = sublayer(tokens, fine_qkv, fine_out, fine_scale, fine_table, fine_gain, shifts[0], bias_index, HEADS)
    rows, columns, width = fine_after.shape
    quads = fine_after.reshape(rows // 2, 2, columns // 2, 2, width).transpose(0, 2, 3, 1, 4).reshape(-1, 4 * width)
    merged = jnp.dot(quads, merge_weight, preferred_element_type=jnp.float32)
    coarse = layer_norm(merged, merge_gain).astype(jnp.bfloat16).reshape(rows // 2, columns // 2, -1)
    coarse_after = sublayer(coarse, coarse_qkv, coarse_out, coarse_scale, coarse_table, coarse_gain, shifts[1], bias_index, HEADS2)
    upward = jnp.repeat(jnp.repeat(coarse_after, 2, axis=0), 2, axis=1)
    return (fine_after.astype(jnp.float32) + upward.astype(jnp.float32)).astype(jnp.bfloat16)
```

```python
import functools

import jax
import jax.numpy as jnp
import numpy as np
from jax import lax
from jax.experimental import pallas as pl
from jax.experimental.pallas import tpu as pltpu
from jax.sharding import PartitionSpec as P

MESH = pl.DeviceIdType.MESH
HEADS = 8
WLAT = 6
WLON = 12
WIN = 72
PAD = 80
D = 512
BF = jnp.bfloat16
F32 = jnp.float32

OWN, LEFT, RIGHT = 0, 288, 432
ABOVE, ABOVE_C, BELOW, BELOW_C = 576, 704, 816, 944
POOL = 1056
CPOOL = 720
NOWHERE = -200000
UNUSED = -100000


def code(row, column):
    return (row + 32) * 128 + column + 32


def padded_codes(places, length, fill):
    out = np.full((length,), fill, np.int32)
    out[: len(places)] = [code(r, c) for r, c in places]
    return out


def grid_places(rows, columns):
    return [(r, c) for r in rows for c in columns]


def frame_places(down, across):
    parts = []
    for a in range(down):
        for b in range(across):
            rows = range(WLAT * a - WLAT, WLAT * a)
            columns = range(WLON * b - WLON, WLON * b)
            parts.append(grid_places(rows, columns))
    return parts


def blocks_of(parts, block, fill):
    return np.concatenate([padded_codes(p, block, fill) for p in parts])


def code_tables():
    own = grid_places(range(12), range(24))
    far_left = grid_places(range(12), range(-11, 0))
    far_right = grid_places(range(12), range(24, 35))
    sides = list(range(-11, 0)) + list(range(24, 35))
    above, below = range(-5, 0), range(12, 17)
    pool = np.concatenate(
        [
            padded_codes(own, 288, NOWHERE),
            padded_codes(far_left, 144, NOWHERE),
            padded_codes(far_right, 144, NOWHERE),
            padded_codes(grid_places(above, range(24)), 128, NOWHERE),
            padded_codes(grid_places(above, sides), 112, NOWHERE),
            padded_codes(grid_places(below, range(24)), 128, NOWHERE),
            padded_codes(grid_places(below, sides), 112, NOWHERE),
        ]
    )
    quads = [
        [(2 * a + i, 2 * b + j) for a in range(6) for b in range(12)]
        for j in range(2)
        for i in range(2)
    ]
    coarse_pool = [
        grid_places(range(6 * down, 6 * down + 6), range(12 * across, 12 * across + 12))
        for down in (0, -1, 1)
        for across in (0, -1, 1)
    ]
    fine_frame, coarse_frame = frame_places(3, 3), frame_places(2, 2)
    by_row = np.full((8, 1152), NOWHERE, np.int32)
    for at, values in enumerate(
        [
            pool,
            blocks_of(fine_frame, PAD, NOWHERE),
            blocks_of(quads, PAD, NOWHERE),
            blocks_of(coarse_pool, PAD, NOWHERE),
            blocks_of(coarse_frame, PAD, NOWHERE),
        ]
    ):
        by_row[at, : len(values)] = values
    by_column = np.full((720, 128), UNUSED, np.int32)
    for at, values in enumerate(
        [
            blocks_of(fine_frame, PAD, UNUSED),
            blocks_of(quads, PAD, UNUSED),
            blocks_of(coarse_frame, PAD, UNUSED),
            blocks_of([grid_places(range(6), range(12))], PAD, UNUSED),
            padded_codes(own, 288, UNUSED),
            padded_codes(grid_places(range(12), range(13, 24)), 144, UNUSED),
            padded_codes(grid_places(range(12), range(11)), 144, UNUSED),
            padded_codes(grid_places(range(7, 12), range(24)), 128, UNUSED),
            padded_codes(grid_places(range(5), range(24)), 128, UNUSED),
            padded_codes(grid_places(range(7, 12), sides), 112, UNUSED),
            padded_codes(grid_places(range(5), sides), 112, UNUSED),
        ]
    ):
        by_column[: len(values), at] = values
    return by_row, by_column


def norm_rows(values, gain):
    middle = jnp.mean(values, axis=-1, keepdims=True)
    centered = values - middle
    spread = jnp.mean(centered * centered, axis=-1, keepdims=True)
    return centered * lax.rsqrt(spread + 1e-05) * gain


def dot(a, b):
    return jnp.dot(a, b, preferred_element_type=F32)


def dot_nt(a, b):
    return lax.dot_general(a, b, (((1,), (1,)), ((), ())), preferred_element_type=F32)


def kernel(
    shifts,
    fine_scale,
    coarse_scale,
    tokens,
    w_fine_qkv,
    w_fine_out,
    w_merge,
    w_coarse_qkv,
    w_coarse_out,
    tables,
    bias_index,
    gains,
    by_row,
    by_column,
    out,
    fine_qkv,
    fine_out,
    merge,
    coarse_qkv,
    coarse_out,
    pool,
    to_right,
    to_left,
    to_below,
    to_above,
    to_below_c,
    to_above_c,
    query,
    key,
    value,
    mixed,
    fine_after,
    coarse_pool,
    bias,
    send_sem,
    recv_sem,
    local_sem,
):
    lat, lon = lax.axis_index("lat"), lax.axis_index("lon")
    core, z_lo = lat % 2, lat // 2
    x, z_hi, y = lon // 8, (lon // 4) % 2, lon % 4
    z = z_hi * 8 + z_lo

    def place(x, y, z, core):
        x, y, z = (x + 4) % 4, (y + 4) % 4, (z + 16) % 16
        return ((z % 8) * 2 + core, x * 8 + (z // 8) * 4 + y)

    def along_z(d):
        return place(x, y, z + d, core)

    def along_x(d):
        return place(x + d, y, z, core)

    def along_y(d):
        return place(x, y + d, z, core)

    line = z * 2 + core

    def along_lat(d):
        spot = (line + d + 32) % 32
        return place(x, y, spot // 2, spot % 2)

    def along_lon(d):
        return (lat, (lon + d + 32) % 32)

    sibling = place(x, y, z, 1 - core)
    opposite = 4 - 8 * core
    hops = (opposite, 3, -3, 2, -2, 1, -1)

    barrier = pltpu.get_barrier_semaphore()
    senders = [along_z(-d) for d in hops]
    senders += [along_x(d) for d in (1, -1, 2)] + [along_y(d) for d in (1, -1, 2)]
    senders += [sibling, along_lon(1), along_lon(-1), along_lat(1), along_lat(-1)]
    for device in senders:
        pl.semaphore_signal(barrier, inc=1, device_id=device, device_id_type=MESH)

    def picked(column, rows, row_at, first, width, offset=0):
        left = by_column[0:rows, column : column + 1] + offset
        right = by_row[row_at : row_at + 1, first : first + width]
        return jnp.where(left == right, 1.0, 0.0).astype(BF)

    own = tokens[...]
    to_right[...] = dot(picked(5, 144, 0, OWN, 288), own).astype(BF)
    to_left[...] = dot(picked(6, 144, 0, OWN, 288), own).astype(BF)
    to_below[...] = dot(picked(7, 128, 0, OWN, 288), own).astype(BF)
    to_above[...] = dot(picked(8, 128, 0, OWN, 288), own).astype(BF)
    pool[OWN : OWN + 288, :] = own

    table = tables[...]
    top = table.astype(BF)
    rest = table - top.astype(F32)
    middle = rest.astype(BF)
    bottom = (rest - middle.astype(F32)).astype(BF)
    table_parts = jnp.concatenate([top, middle, bottom], axis=0)
    levels = lax.broadcasted_iota(jnp.int32, (256, 128), 0)

    def bias_rows(group, carry):
        rows = bias_index[pl.ds(pl.multiple_of(group * 8, 8), 8), :]
        for i in range(8):
            hot = jnp.where(levels == rows[i : i + 1, :], 1.0, 0.0).astype(BF)
            parts = dot(table_parts, hot)
            looked = parts[0:16] + parts[16:32] + parts[32:48]
            bias[:, pl.ds(group * 8 + i, 1), :] = looked.reshape(16, 1, 128)
        return carry

    lax.fori_loop(0, PAD // 8, bias_rows, 0)

    counter = [0]
    sent = []

    def send(source, target, device):
        at = counter[0]
        counter[0] += 1
        copy = pltpu.make_async_remote_copy(
            src_ref=source,
            dst_ref=target,
            send_sem=send_sem.at[at],
            recv_sem=recv_sem.at[at],
            device_id=device,
            device_id_type=MESH,
        )
        copy.start()
        sent.append(copy)
        return copy

    def arrived(copies):
        for copy in copies:
            copy.wait_recv()

    pl.semaphore_wait(barrier, len(senders))

    side_copies = [
        send(to_right, pool.at[pl.ds(LEFT, 144)], along_lon(1)),
        send(to_left, pool.at[pl.ds(RIGHT, 144)], along_lon(-1)),
    ]
    row_copies = [
        send(to_below, pool.at[pl.ds(ABOVE, 128)], along_lat(1)),
        send(to_above, pool.at[pl.ds(BELOW, 128)], along_lat(-1)),
    ]

    def corner(g, first, width):
        rows = pl.ds(pl.multiple_of((g // 2) * 16, 16), 16)
        return rows, pl.ds(pl.multiple_of(first + (g % 2) * width, 128), width)

    def band(g, first, width):
        return pl.ds(pl.multiple_of(g * 32, 32), 32), pl.ds(first, width)

    local_count = [0]

    class Gather:
        def __init__(self, shard, whole, halves):
            self.shard, self.whole, self.halves = shard, whole, halves

        def start(self):
            self.own, self.first = [], []
            for axis, (rows, columns) in self.halves:
                at = local_count[0]
                local_count[0] += 1
                copy = pltpu.make_async_copy(
                    self.shard.at[rows, columns],
                    self.whole.at[z_lo, core, rows, columns],
                    local_sem.at[at],
                )
                copy.start()
                self.own.append(copy)
                for d in hops:
                    self.first.append(
                        send(
                            self.shard.at[rows, columns],
                            self.whole.at[z_lo, core, rows, columns],
                            along_z(d),
                        )
                    )

        def spread(self):
            for copy in self.own:
                copy.wait()
            arrived(self.first)
            self.second = []
            for axis, (rows, columns) in self.halves:
                for d in (1, -1, 2):
                    part = self.whole.at[:, core, rows, columns]
                    self.second.append(send(part, part, axis(d)))

        def share(self):
            arrived(self.second)
            part = self.whole.at[:, core]
            self.third = [send(part, part, sibling)]

        def finish(self):
            arrived(self.third)

    wide_halves = [(along_x, corner(x, 0, 384)), (along_y, corner(y, 768, 384))]
    g_fine_qkv = Gather(w_fine_qkv, fine_qkv, wide_halves)
    g_fine_out = Gather(w_fine_out, fine_out, [(along_x, corner(x, 0, 256))])
    g_merge = Gather(w_merge, merge, [(along_x, band(x, 0, 256)), (along_y, band(y, 256, 256))])
    g_coarse_qkv = Gather(w_coarse_qkv, coarse_qkv, wide_halves)
    g_coarse_out = Gather(w_coarse_out, coarse_out, [(along_y, corner(y, 0, 256))])

    g_fine_qkv.start()
    g_fine_out.start()
    g_merge.start()
    g_fine_qkv.spread()
    g_fine_qkv.share()
    g_fine_out.spread()
    g_merge.spread()

    arrived(side_copies)
    sides = pool[LEFT : LEFT + 288, :]
    own_sides = pool[OWN : OWN + 576, :]
    to_below_c[...] = dot(picked(9, 112, 0, OWN, 576), own_sides).astype(BF)
    to_above_c[...] = dot(picked(10, 112, 0, OWN, 576), own_sides).astype(BF)
    row_copies += [
        send(to_below_c, pool.at[pl.ds(ABOVE_C, 112)], along_lat(1)),
        send(to_above_c, pool.at[pl.ds(BELOW_C, 112)], along_lat(-1)),
    ]
    g_fine_out.share()
    g_merge.share()
    g_coarse_qkv.start()
    g_coarse_out.start()

    lane = lax.broadcasted_iota(jnp.int32, (1, 128), 1)
    low = jnp.where(lane < 64, 1.0, 0.0).astype(BF)
    high = jnp.where(lane < 64, 0.0, 1.0).astype(BF)
    row_of = jnp.zeros((1, 128), jnp.int32)
    for r in range(1, WLAT):
        row_of = row_of + jnp.where(lane >= WLON * r, 1, 0)
    ones_row = lax.broadcasted_iota(jnp.int32, (256, 256), 0) // 64
    ones_column = lax.broadcasted_iota(jnp.int32, (256, 256), 1) // 64
    same_head = jnp.where(ones_row == ones_column, 1.0, 0.0).astype(BF)

    def scale_row(scale):
        head_of = lax.broadcasted_iota(jnp.int32, (1, D), 1) // 64
        row = jnp.zeros((1, D), F32)
        for n in range(HEADS):
            row = jnp.where(head_of == n, scale[n], row)
        return row

    def project(level, across, down, column, row_at, cells, width, weights, scale):
        offset = shifts[level, 0] * 128 + shifts[level, 1]
        scales = scale_row(scale)
        tall = across * PAD

        def one(a, carry):
            at = pl.multiple_of(a * tall, tall)
            left = by_column[pl.ds(at, tall), column : column + 1] + offset
            right = by_row[row_at : row_at + 1, 0:width]
            hot = jnp.where(left == right, 1.0, 0.0).astype(BF)
            frame = dot(hot, cells[...]).astype(BF)
            for n in range(6):
                block = weights[:, :, :, 256 * n : 256 * n + 256].reshape(D, 256)
                rounded = dot(frame, block).astype(BF)
                where_to = pl.ds(a * across, across)
                columns = slice(256 * (n % 2), 256 * (n % 2) + 256)
                if n < 4:
                    full = rounded.astype(F32)
                    square = dot((full * full).astype(BF), same_head)
                    full = full * lax.rsqrt(square + 1e-06)
                    if n < 2:
                        full = full * scales[:, columns]
                    rounded = full.astype(BF)
                target = (query, key, value)[n // 2]
                target[where_to, :, columns] = rounded.reshape(across, PAD, 256)
            return carry

        lax.fori_loop(0, down, one, 0)

    def attend(level, across, down, rows_here):
        first_row = lat * rows_here + shifts[level, 0] - WLAT

        def one(w, carry):
            latitude = row_of + (first_row + WLAT * (w // across))
            here = (latitude >= 0) & (latitude < rows_here * 16) & (lane < WIN)
            keep = jnp.where(here, 1.0, 0.0)[:, 0:PAD]
            for p in range(HEADS // 2):
                columns = slice(128 * p, 128 * p + 128)
                q = query[w, :, columns]
                pair = jnp.concatenate([q * low, q * high], axis=0)
                scores = dot_nt(pair, key[w, :, columns])
                own_bias = bias[8 * level + 2 * p : 8 * level + 2 * p + 2, :, 0:PAD]
                powers = jnp.exp(scores + own_bias.reshape(2 * PAD, PAD)) * keep
                total = jnp.sum(powers, axis=-1, keepdims=True)
                weights = (powers * (1.0 / total)).astype(BF)
                both = dot(weights, value[w, :, columns])
                taken = jnp.where(lane < 64, both[0:PAD], both[PAD : 2 * PAD])
                mixed[w, :, columns] = taken.astype(BF)
            return carry

        lax.fori_loop(0, across * down, one, 0)

    def finish(level, windows, column, rows, row_at, weights, base, gain):
        offset = shifts[level, 0] * 128 + shifts[level, 1]
        left = by_column[0:rows, column : column + 1] - offset
        right = by_row[row_at : row_at + 1, 0 : windows * PAD]
        hot = jnp.where(left == right, 1.0, 0.0).astype(BF)
        taken = dot(hot, mixed[0:windows].reshape(windows * PAD, D)).astype(BF)
        branch = dot(taken, weights[...].reshape(D, D))
        return (base + norm_rows(branch, gain)).astype(BF)

    g_fine_qkv.finish()
    arrived(row_copies)
    project(0, 3, 3, 0, 0, pool, POOL, fine_qkv, fine_scale)
    attend(0, 3, 3, 12)
    g_coarse_qkv.spread()
    g_coarse_out.spread()
    g_fine_out.finish()
    in_quads = dot(picked(1, 320, 0, OWN, 288), tokens[...])
    fine_after[...] = finish(0, 9, 1, 320, 1, fine_out, in_quads, gains[0:1, :])
    g_merge.finish()
    merged = jnp.zeros((PAD, D), F32)
    for p in range(4):
        rows = merge[2 * p : 2 * p + 2].reshape(D, D)
        merged = merged + dot(fine_after[PAD * p : PAD * p + PAD, :], rows)
    coarse_pool[0:PAD, :] = norm_rows(merged, gains[1:2, :]).astype(BF)
    mine = coarse_pool.at[pl.ds(0, PAD)]
    side_copies = [
        send(mine, coarse_pool.at[pl.ds(PAD, PAD)], along_lon(1)),
        send(mine, coarse_pool.at[pl.ds(2 * PAD, PAD)], along_lon(-1)),
    ]
    g_coarse_qkv.share()
    g_coarse_out.share()
    arrived(side_copies)
    three = coarse_pool.at[pl.ds(0, 3 * PAD)]
    row_copies = [
        send(three, coarse_pool.at[pl.ds(3 * PAD, 3 * PAD)], along_lat(1)),
        send(three, coarse_pool.at[pl.ds(6 * PAD, 3 * PAD)], along_lat(-1)),
    ]
    g_coarse_qkv.finish()
    arrived(row_copies)
    project(1, 2, 2, 2, 3, coarse_pool, CPOOL, coarse_qkv, coarse_scale)
    attend(1, 2, 2, 6)
    g_coarse_out.finish()
    base = coarse_pool[0:PAD, :].astype(F32)
    coarse_after = finish(1, 4, 3, PAD, 4, coarse_out, base, gains[2:3, :]).astype(F32)
    for p in range(4):
        part = fine_after[PAD * p : PAD * p + PAD, :].astype(F32) + coarse_after
        fine_after[PAD * p : PAD * p + PAD, :] = part.astype(BF)
    out[...] = dot(picked(4, 288, 2, 0, 320), fine_after[...]).astype(BF)
    for copy in sent:
        copy.wait_send()


COPIES = 4 + 2 + 4 + 3 * 21 + 2 * 11


def per_device(
    tokens,
    fine_qkv,
    fine_out,
    fine_scale,
    fine_table,
    fine_gain,
    merge_weight,
    merge_gain,
    coarse_qkv,
    coarse_out,
    coarse_scale,
    coarse_table,
    coarse_gain,
    shifts,
    bias_index,
):
    by_row, by_column = code_tables()
    tables = jnp.concatenate([fine_table, coarse_table], axis=1)
    tables = jnp.pad(tables, ((0, 3), (0, 0))).T
    index = jnp.pad(bias_index, ((0, 8), (0, 56)), constant_values=255)
    gains = jnp.stack([fine_gain, merge_gain, coarse_gain])
    rows, columns, width = tokens.shape
    smem = pl.BlockSpec(memory_space=pltpu.SMEM)
    vmem = pl.BlockSpec(memory_space=pltpu.VMEM)
    anywhere = pl.BlockSpec(memory_space=pl.ANY)
    result = pl.pallas_call(
        kernel,
        out_shape=jax.ShapeDtypeStruct((rows * columns, width), BF),
        in_specs=[smem] * 3 + [vmem] + [anywhere] * 5 + [vmem] * 5,
        out_specs=vmem,
        scratch_shapes=[
            pltpu.VMEM((8, 2, 32, 1536), BF),
            pltpu.VMEM((8, 2, 32, 512), BF),
            pltpu.VMEM((8, 2, 128, 512), BF),
            pltpu.VMEM((8, 2, 32, 1536), BF),
            pltpu.VMEM((8, 2, 32, 512), BF),
            pltpu.VMEM((POOL, D), BF),
            pltpu.VMEM((144, D), BF),
            pltpu.VMEM((144, D), BF),
            pltpu.VMEM((128, D), BF),
            pltpu.VMEM((128, D), BF),
            pltpu.VMEM((112, D), BF),
            pltpu.VMEM((112, D), BF),
            pltpu.VMEM((9, PAD, D), BF),
            pltpu.VMEM((9, PAD, D), BF),
            pltpu.VMEM((9, PAD, D), BF),
            pltpu.VMEM((9, PAD, D), BF),
            pltpu.VMEM((320, D), BF),
            pltpu.VMEM((CPOOL, D), BF),
            pltpu.VMEM((16, PAD, 128), F32),
            pltpu.SemaphoreType.DMA((COPIES,)),
            pltpu.SemaphoreType.DMA((COPIES,)),
            pltpu.SemaphoreType.DMA((8,)),
        ],
        compiler_params=pltpu.CompilerParams(
            collective_id=0, has_side_effects=True, vmem_limit_bytes=48 << 20
        ),
    )(
        shifts,
        fine_scale,
        coarse_scale,
        tokens.reshape(rows * columns, width),
        fine_qkv,
        fine_out,
        merge_weight,
        coarse_qkv,
        coarse_out,
        tables,
        index,
        gains,
        jnp.asarray(by_row),
        jnp.asarray(by_column),
    )
    return result.reshape(rows, columns, width)


def solution(mesh):
    placed = (
        P("lat", "lon", None),
        P("lat", None),
        P("lat", None),
        P(),
        P(),
        P(),
        P("lat", None),
        P(),
        P("lat", None),
        P("lat", None),
        P(),
        P(),
        P(),
        P(),
        P(),
    )
    return jax.shard_map(
        per_device, mesh=mesh, in_specs=placed, out_specs=P("lat", "lon", None), check_vma=False
    )
```

```python
import functools

import jax
import jax.numpy as jnp
import numpy as np
from jax import lax
from jax.experimental import pallas as pl
from jax.experimental.pallas import tpu as pltpu
from jax.sharding import PartitionSpec as P

MESH = pl.DeviceIdType.MESH
HEADS = 8
WLAT = 6
WLON = 12
WIN = 72
PAD = 80
D = 512
BF = jnp.bfloat16
F32 = jnp.float32

ABOVE, BELOW, OWN, LEFT, RIGHT, ABOVE_C, BELOW_C = 0, 128, 256, 544, 688, 832, 944
POOL = 1056
C_LEFT, C_RIGHT, C_ABOVE, C_BELOW, C_ABOVE_C, C_BELOW_C = 80, 160, 240, 320, 400, 512
CPOOL = 624
FINE_WINDOWS = [(0, 1), (1, 1), (2, 1), (1, 0), (1, 2), (0, 0), (0, 2), (2, 0), (2, 2)]
COARSE_WINDOWS = [(0, 0), (0, 1), (1, 0), (1, 1)]
NOWHERE = -200000
UNUSED = -100000


def code(row, column):
    return (row + 32) * 128 + column + 32


def padded_codes(places, length, fill):
    out = np.full((length,), fill, np.int32)
    out[: len(places)] = [code(r, c) for r, c in places]
    return out


def grid_places(rows, columns):
    return [(r, c) for r in rows for c in columns]


def frame_places(windows):
    parts = []
    for a, b in windows:
        rows = range(WLAT * a - WLAT, WLAT * a)
        columns = range(WLON * b - WLON, WLON * b)
        parts.append(grid_places(rows, columns))
    return parts


def blocks_of(parts, block, fill):
    return np.concatenate([padded_codes(p, block, fill) for p in parts])


def code_tables():
    own = grid_places(range(12), range(24))
    far_left = grid_places(range(12), range(-11, 0))
    far_right = grid_places(range(12), range(24, 35))
    sides = list(range(-11, 0)) + list(range(24, 35))
    above, below = range(-5, 0), range(12, 17)
    pool = np.concatenate(
        [
            padded_codes(grid_places(above, range(24)), 128, NOWHERE),
            padded_codes(grid_places(below, range(24)), 128, NOWHERE),
            padded_codes(own, 288, NOWHERE),
            padded_codes(far_left, 144, NOWHERE),
            padded_codes(far_right, 144, NOWHERE),
            padded_codes(grid_places(above, sides), 112, NOWHERE),
            padded_codes(grid_places(below, sides), 112, NOWHERE),
        ]
    )
    quads = [
        [(2 * a + i, 2 * b + j) for a in range(6) for b in range(12)]
        for j in range(2)
        for i in range(2)
    ]
    coarse_sides = list(range(-11, 0)) + list(range(12, 23))
    coarse_tiles = [(0, 0), (0, -1), (0, 1), (-1, 0), (1, 0)]
    coarse_pool = np.concatenate(
        [
            padded_codes(
                grid_places(range(6 * i, 6 * i + 6), range(12 * j, 12 * j + 12)), PAD, NOWHERE
            )
            for i, j in coarse_tiles
        ]
        + [
            padded_codes(grid_places(range(-5, 0), coarse_sides), 112, NOWHERE),
            padded_codes(grid_places(range(6, 11), coarse_sides), 112, NOWHERE),
        ]
    )
    fine_frame, coarse_frame = frame_places(FINE_WINDOWS), frame_places(COARSE_WINDOWS)
    by_row = np.full((8, 1152), NOWHERE, np.int32)
    for at, values in enumerate(
        [
            pool,
            blocks_of(fine_frame, PAD, NOWHERE),
            blocks_of(quads, PAD, NOWHERE),
            coarse_pool,
            blocks_of(coarse_frame, PAD, NOWHERE),
        ]
    ):
        by_row[at, : len(values)] = values
    by_column = np.full((720, 128), UNUSED, np.int32)
    for at, values in enumerate(
        [
            blocks_of(fine_frame, PAD, UNUSED),
            blocks_of(quads, PAD, UNUSED),
            blocks_of(coarse_frame, PAD, UNUSED),
            blocks_of([grid_places(range(6), range(12))], PAD, UNUSED),
            padded_codes(own, 288, UNUSED),
            padded_codes(grid_places(range(12), range(13, 24)), 144, UNUSED),
            padded_codes(grid_places(range(12), range(11)), 144, UNUSED),
            padded_codes(grid_places(range(7, 12), range(24)), 128, UNUSED),
            padded_codes(grid_places(range(5), range(24)), 128, UNUSED),
            padded_codes(grid_places(range(7, 12), sides), 112, UNUSED),
            padded_codes(grid_places(range(5), sides), 112, UNUSED),
            padded_codes(grid_places(range(1, 6), coarse_sides), 112, UNUSED),
            padded_codes(grid_places(range(5), coarse_sides), 112, UNUSED),
        ]
    ):
        by_column[: len(values), at] = values
    return by_row, by_column


def norm_rows(values, gain):
    middle = jnp.mean(values, axis=-1, keepdims=True)
    centered = values - middle
    spread = jnp.mean(centered * centered, axis=-1, keepdims=True)
    return centered * lax.rsqrt(spread + 1e-05) * gain


def dot(a, b):
    return jnp.dot(a, b, preferred_element_type=F32)


def dot_nt(a, b):
    return lax.dot_general(a, b, (((1,), (1,)), ((), ())), preferred_element_type=F32)


def kernel(
    shifts,
    fine_scale,
    coarse_scale,
    hbm_tokens,
    w_fine_qkv,
    w_fine_out,
    w_merge,
    w_coarse_qkv,
    w_coarse_out,
    hbm_fine_table,
    hbm_coarse_table,
    hbm_bias_index,
    hbm_fine_gain,
    hbm_merge_gain,
    hbm_coarse_gain,
    hbm_by_row,
    hbm_by_column,
    out,
    fine_qkv,
    fine_out,
    merge,
    coarse_qkv,
    coarse_out,
    pool,
    to_right,
    to_left,
    to_below,
    to_above,
    to_below_c,
    to_above_c,
    query,
    key,
    value,
    mixed,
    fine_after,
    coarse_pool,
    bias,
    tokens,
    fine_table,
    coarse_table,
    bias_index,
    fine_gain,
    merge_gain,
    coarse_gain,
    by_row,
    by_column,
    tables,
    to_below_k,
    to_above_k,
    send_sem,
    recv_sem,
    local_sem,
):
    lat, lon = lax.axis_index("lat"), lax.axis_index("lon")
    core, z_lo = lat % 2, lat // 2
    x, z_hi, y = lon // 8, (lon // 4) % 2, lon % 4
    z = z_hi * 8 + z_lo

    def place(x, y, z, core):
        x, y, z = (x + 4) % 4, (y + 4) % 4, (z + 16) % 16
        return ((z % 8) * 2 + core, x * 8 + (z // 8) * 4 + y)

    def along_z(d):
        return place(x, y, z + d, core)

    def along_x(d):
        return place(x + d, y, z, core)

    def along_y(d):
        return place(x, y + d, z, core)

    line = z * 2 + core

    def along_lat(d):
        spot = (line + d + 32) % 32
        return place(x, y, spot // 2, spot % 2)

    def along_lon(d):
        return (lat, (lon + d + 32) % 32)

    sibling = place(x, y, z, 1 - core)
    opposite = 4 - 8 * core
    hops = (opposite, 3, -3, 2, -2, 1, -1)

    barrier = pltpu.get_barrier_semaphore()
    senders = [along_z(-d) for d in hops]
    senders += [along_x(d) for d in (1, -1, 2)] + [along_y(d) for d in (1, -1, 2)]
    senders += [sibling, along_lon(1), along_lon(-1), along_lat(1), along_lat(-1)]
    for device in senders:
        pl.semaphore_signal(barrier, inc=1, device_id=device, device_id_type=MESH)

    local_count = [0]

    def bring(source, target):
        at = local_count[0]
        local_count[0] += 1
        copy = pltpu.make_async_copy(source, target, local_sem.at[at])
        copy.start()
        return copy

    first = [
        bring(hbm_tokens, tokens),
        bring(hbm_by_row, by_row),
        bring(hbm_by_column, by_column),
    ]
    later = [
        bring(hbm_fine_table, fine_table),
        bring(hbm_coarse_table, coarse_table),
        bring(hbm_bias_index, bias_index),
        bring(hbm_fine_gain, fine_gain),
        bring(hbm_merge_gain, merge_gain),
        bring(hbm_coarse_gain, coarse_gain),
    ]

    def picked(column, rows, row_at, first, width, offset=0):
        left = by_column[0:rows, column : column + 1] + offset
        right = by_row[row_at : row_at + 1, first : first + width]
        return jnp.where(left == right, 1.0, 0.0).astype(BF)

    counter = [0]
    sent = []

    def send(source, target, device):
        at = counter[0]
        counter[0] += 1
        copy = pltpu.make_async_remote_copy(
            src_ref=source,
            dst_ref=target,
            send_sem=send_sem.at[at],
            recv_sem=recv_sem.at[at],
            device_id=device,
            device_id_type=MESH,
        )
        copy.start()
        sent.append(copy)
        return copy

    def arrived(copies):
        for copy in copies:
            copy.wait_recv()

    class Gather:
        def __init__(self, shard, whole, halves):
            self.shard, self.whole, self.halves = shard, whole, halves

        def start(self):
            self.ready, self.waits = [], []
            for axis, part, pair_axis, small in self.halves:
                rows, columns = small
                source = self.shard.at[rows, columns]
                target = self.whole.at[z_lo, core, rows, columns]
                self.ready.append(bring(source, target))
                for d in hops:
                    self.waits.append(send(source, target, along_z(d)))

        def begun(self):
            for copy in self.ready:
                copy.wait()
            arrived(self.waits)
            self.ready, self.waits = [], []

        def pair(self):
            self.begun()
            for axis, part, pair_axis, (rows, columns) in self.halves:
                area = self.whole.at[:, core, rows, columns]
                self.waits.append(send(area, area, pair_axis(1)))

        def spread(self):
            self.begun()
            for axis, (rows, columns), pair_axis, small in self.halves:
                area = self.whole.at[:, core, rows, columns]
                for d in (1, -1, 2):
                    self.waits.append(send(area, area, axis(d)))

        def share(self):
            arrived(self.waits)
            part = self.whole.at[:, core]
            self.waits = [send(part, part, sibling)]

        def finish(self):
            arrived(self.waits)

    def by_x(part):
        return along_x, part(x), along_y, part(x, y % 2)

    def by_y(part):
        return along_y, part(y), along_x, part(y, x % 2)

    def corner(first, width):
        def part(g, half=None):
            rows = pl.ds(pl.multiple_of((g // 2) * 16, 16), 16)
            at, wide = first + (g % 2) * width, width
            if half is not None:
                at, wide = at + half * (width // 2), width // 2
            return rows, pl.ds(pl.multiple_of(at, 128), wide)

        return part

    def band(first, width):
        def part(g, half=None):
            if half is None:
                return pl.ds(pl.multiple_of(g * 32, 32), 32), pl.ds(first, width)
            return pl.ds(pl.multiple_of(g * 32 + half * 16, 16), 16), pl.ds(first, width)

        return part

    def quarters(axis, g, first):
        part = corner(first, 384)(g)
        return axis, part, None, part

    g_fine_qkv = Gather(
        w_fine_qkv, fine_qkv, [quarters(along_x, x, 0), quarters(along_y, y, 768)]
    )
    g_fine_out = Gather(w_fine_out, fine_out, [by_x(corner(0, 256))])
    g_merge = Gather(w_merge, merge, [by_x(band(0, 256)), by_y(band(256, 256))])
    g_coarse_qkv = Gather(w_coarse_qkv, coarse_qkv, [by_x(corner(0, 768))])
    g_coarse_out = Gather(w_coarse_out, coarse_out, [by_y(corner(0, 256))])

    pl.semaphore_wait(barrier, len(senders))
    g_fine_qkv.start()
    g_fine_out.start()
    g_merge.start()
    for copy in first:
        copy.wait()
    own = tokens[...]
    to_right[...] = dot(picked(5, 144, 0, OWN, 288), own).astype(BF)
    to_left[...] = dot(picked(6, 144, 0, OWN, 288), own).astype(BF)
    to_below[...] = dot(picked(7, 128, 0, OWN, 288), own).astype(BF)
    to_above[...] = dot(picked(8, 128, 0, OWN, 288), own).astype(BF)
    pool[OWN : OWN + 288, :] = own

    bias[...] = jnp.zeros((16, PAD, 128), F32)
    tables[...] = jnp.zeros((16, 256), F32)
    for copy in later:
        copy.wait()
    tables[0:HEADS, 0:253] = fine_table[...]
    tables[HEADS : 2 * HEADS, 0:253] = coarse_table[...]
    table = tables[...]
    top = table.astype(BF)
    rest = table - top.astype(F32)
    middle = rest.astype(BF)
    bottom = (rest - middle.astype(F32)).astype(BF)
    table_parts = jnp.concatenate([top, middle, bottom], axis=0)
    levels = lax.broadcasted_iota(jnp.int32, (256, WIN), 0)

    def bias_rows(group, carry):
        rows = bias_index[pl.ds(pl.multiple_of(group * 8, 8), 8), :]
        for i in range(8):
            hot = jnp.where(levels == rows[i : i + 1, :], 1.0, 0.0).astype(BF)
            parts = dot(table_parts, hot)
            looked = parts[0:16] + parts[16:32] + parts[32:48]
            bias[:, pl.ds(group * 8 + i, 1), 0:WIN] = looked.reshape(16, 1, WIN)
        return carry

    lax.fori_loop(0, WIN // 8, bias_rows, 0)

    g_fine_qkv.spread()
    side_copies = [
        send(to_right, pool.at[pl.ds(LEFT, 144)], along_lon(1)),
        send(to_left, pool.at[pl.ds(RIGHT, 144)], along_lon(-1)),
    ]
    row_copies = [
        send(to_below, pool.at[pl.ds(ABOVE, 128)], along_lat(1)),
        send(to_above, pool.at[pl.ds(BELOW, 128)], along_lat(-1)),
    ]
    g_fine_qkv.share()
    g_fine_out.pair()
    g_merge.pair()

    lane = lax.broadcasted_iota(jnp.int32, (1, 128), 1)
    low = jnp.where(lane < 64, 1.0, 0.0).astype(BF)
    high = jnp.where(lane < 64, 0.0, 1.0).astype(BF)
    row_of = jnp.zeros((1, 128), jnp.int32)
    for r in range(1, WLAT):
        row_of = row_of + jnp.where(lane >= WLON * r, 1, 0)
    ones_row = lax.broadcasted_iota(jnp.int32, (256, 256), 0) // 64
    ones_column = lax.broadcasted_iota(jnp.int32, (256, 256), 1) // 64
    same_head = jnp.where(ones_row == ones_column, 1.0, 0.0).astype(BF)

    def scale_row(scale):
        head_of = lax.broadcasted_iota(jnp.int32, (1, D), 1) // 64
        row = jnp.zeros((1, D), F32)
        for n in range(HEADS):
            row = jnp.where(head_of == n, scale[n], row)
        return row

    def project(level, windows, column, row_at, cells, first, width, weights, scale):
        offset = shifts[level, 0] * 128 + shifts[level, 1]
        scales = scale_row(scale)
        at, count = windows
        left = by_column[at * PAD : (at + count) * PAD, column : column + 1] + offset
        right = by_row[row_at : row_at + 1, first : first + width]
        hot = jnp.where(left == right, 1.0, 0.0).astype(BF)
        frame = dot(hot, cells[first : first + width, :]).astype(BF)
        for n in range(6):
            block = weights[:, :, :, 256 * n : 256 * n + 256].reshape(D, 256)
            rounded = dot(frame, block).astype(BF)
            columns = slice(256 * (n % 2), 256 * (n % 2) + 256)
            if n < 4:
                full = rounded.astype(F32)
                square = dot((full * full).astype(BF), same_head)
                full = full * lax.rsqrt(square + 1e-06)
                if n < 2:
                    full = full * scales[:, columns]
                rounded = full.astype(BF)
            target = (query, key, value)[n // 2]
            target[at : at + count, :, columns] = rounded.reshape(count, PAD, 256)

    def attend(level, windows, row_block, rows_here):
        first_row = lat * rows_here + shifts[level, 0] - WLAT
        at, count = windows

        def one(w, carry):
            latitude = row_of + (first_row + WLAT * row_block(w))
            here = (latitude >= 0) & (latitude < rows_here * 16) & (lane < WIN)
            keep = jnp.where(here, 1.0, 0.0)[:, 0:PAD]
            for p in range(HEADS // 2):
                columns = slice(128 * p, 128 * p + 128)
                q = query[at + w, :, columns]
                pair = jnp.concatenate([q * low, q * high], axis=0)
                scores = dot_nt(pair, key[at + w, :, columns])
                own_bias = bias[8 * level + 2 * p : 8 * level + 2 * p + 2, :, 0:PAD]
                powers = jnp.exp(scores + own_bias.reshape(2 * PAD, PAD)) * keep
                total = jnp.sum(powers, axis=-1, keepdims=True)
                weights = (powers * (1.0 / total)).astype(BF)
                both = dot(weights, value[at + w, :, columns])
                taken = jnp.where(lane < 64, both[0:PAD], both[PAD : 2 * PAD])
                mixed[at + w, :, columns] = taken.astype(BF)
            return carry

        lax.fori_loop(0, count, one, 0)

    def finish(level, windows, column, rows, row_at, weights, base, gain):
        offset = shifts[level, 0] * 128 + shifts[level, 1]
        left = by_column[0:rows, column : column + 1] - offset
        right = by_row[row_at : row_at + 1, 0 : windows * PAD]
        hot = jnp.where(left == right, 1.0, 0.0).astype(BF)
        taken = dot(hot, mixed[0:windows].reshape(windows * PAD, D)).astype(BF)
        branch = dot(taken, weights[...].reshape(D, D))
        return (base + norm_rows(branch, gain)).astype(BF)

    g_fine_qkv.finish()
    arrived(row_copies)
    project(0, (0, 3), 0, 0, pool, ABOVE, 544, fine_qkv, fine_scale)
    g_fine_out.spread()
    g_merge.spread()
    attend(0, (0, 3), lambda w: w, 12)

    arrived(side_copies)
    near = pool[OWN : OWN + 576, :]
    to_below_c[...] = dot(picked(9, 112, 0, OWN, 576), near).astype(BF)
    to_above_c[...] = dot(picked(10, 112, 0, OWN, 576), near).astype(BF)
    row_copies = [
        send(to_below_c, pool.at[pl.ds(ABOVE_C, 112)], along_lat(1)),
        send(to_above_c, pool.at[pl.ds(BELOW_C, 112)], along_lat(-1)),
    ]
    g_coarse_qkv.start()
    g_coarse_out.start()
    project(0, (3, 2), 0, 0, pool, OWN, 576, fine_qkv, fine_scale)
    attend(0, (3, 2), lambda w: 1, 12)

    arrived(row_copies)
    project(0, (5, 4), 0, 0, pool, 0, POOL, fine_qkv, fine_scale)
    g_fine_out.share()
    attend(0, (5, 4), lambda w: 2 * (w // 2), 12)
    g_merge.share()
    g_fine_out.finish()
    in_quads = dot(picked(1, 320, 0, OWN, 288), tokens[...])
    fine_after[...] = finish(0, 9, 1, 320, 1, fine_out, in_quads, fine_gain[...])
    g_coarse_qkv.pair()
    g_coarse_out.pair()
    g_merge.finish()
    merged = jnp.zeros((PAD, D), F32)
    for p in range(4):
        rows = merge[2 * p : 2 * p + 2].reshape(D, D)
        merged = merged + dot(fine_after[PAD * p : PAD * p + PAD, :], rows)
    coarse_pool[0:PAD, :] = norm_rows(merged, merge_gain[...]).astype(BF)
    mine = coarse_pool.at[pl.ds(0, PAD)]
    side_copies = [
        send(mine, coarse_pool.at[pl.ds(C_LEFT, PAD)], along_lon(1)),
        send(mine, coarse_pool.at[pl.ds(C_RIGHT, PAD)], along_lon(-1)),
    ]
    row_copies = [
        send(mine, coarse_pool.at[pl.ds(C_ABOVE, PAD)], along_lat(1)),
        send(mine, coarse_pool.at[pl.ds(C_BELOW, PAD)], along_lat(-1)),
    ]
    g_coarse_qkv.spread()
    g_coarse_out.spread()
    arrived(side_copies)
    near = coarse_pool[0 : 3 * PAD, :]
    to_below_k[...] = dot(picked(11, 112, 3, 0, 3 * PAD), near).astype(BF)
    to_above_k[...] = dot(picked(12, 112, 3, 0, 3 * PAD), near).astype(BF)
    row_copies += [
        send(to_below_k, coarse_pool.at[pl.ds(C_ABOVE_C, 112)], along_lat(1)),
        send(to_above_k, coarse_pool.at[pl.ds(C_BELOW_C, 112)], along_lat(-1)),
    ]
    g_coarse_qkv.share()
    g_coarse_out.share()
    g_coarse_qkv.finish()
    arrived(row_copies)
    project(1, (0, 4), 2, 3, coarse_pool, 0, CPOOL, coarse_qkv, coarse_scale)
    attend(1, (0, 4), lambda w: w // 2, 6)
    g_coarse_out.finish()
    base = coarse_pool[0:PAD, :].astype(F32)
    coarse_after = finish(1, 4, 3, PAD, 4, coarse_out, base, coarse_gain[...]).astype(F32)
    for p in range(4):
        part = fine_after[PAD * p : PAD * p + PAD, :].astype(F32) + coarse_after
        fine_after[PAD * p : PAD * p + PAD, :] = part.astype(BF)
    out[...] = dot(picked(4, 288, 2, 0, 320), fine_after[...]).astype(BF)
    for copy in sent:
        copy.wait_send()


COPIES = 12 + 21 + 12 + 23 + 12 + 12


def per_device(
    tokens,
    fine_qkv,
    fine_out,
    fine_scale,
    fine_table,
    fine_gain,
    merge_weight,
    merge_gain,
    coarse_qkv,
    coarse_out,
    coarse_scale,
    coarse_table,
    coarse_gain,
    shifts,
    bias_index,
):
    by_row, by_column = code_tables()
    rows, columns, width = tokens.shape
    smem = pl.BlockSpec(memory_space=pltpu.SMEM)
    vmem = pl.BlockSpec(memory_space=pltpu.VMEM)
    hbm = pl.BlockSpec(memory_space=pltpu.HBM)
    result = pl.pallas_call(
        kernel,
        out_shape=jax.ShapeDtypeStruct((rows * columns, width), BF),
        in_specs=[smem] * 3 + [hbm] * 14,
        out_specs=vmem,
        scratch_shapes=[
            pltpu.VMEM((8, 2, 32, 1536), BF),
            pltpu.VMEM((8, 2, 32, 512), BF),
            pltpu.VMEM((8, 2, 128, 512), BF),
            pltpu.VMEM((8, 2, 32, 1536), BF),
            pltpu.VMEM((8, 2, 32, 512), BF),
            pltpu.VMEM((POOL, D), BF),
            pltpu.VMEM((144, D), BF),
            pltpu.VMEM((144, D), BF),
            pltpu.VMEM((128, D), BF),
            pltpu.VMEM((128, D), BF),
            pltpu.VMEM((112, D), BF),
            pltpu.VMEM((112, D), BF),
            pltpu.VMEM((9, PAD, D), BF),
            pltpu.VMEM((9, PAD, D), BF),
            pltpu.VMEM((9, PAD, D), BF),
            pltpu.VMEM((9, PAD, D), BF),
            pltpu.VMEM((320, D), BF),
            pltpu.VMEM((CPOOL, D), BF),
            pltpu.VMEM((16, PAD, 128), F32),
            pltpu.VMEM((288, D), BF),
            pltpu.VMEM((HEADS, 253), F32),
            pltpu.VMEM((HEADS, 253), F32),
            pltpu.VMEM((WIN, WIN), jnp.int32),
            pltpu.VMEM((1, D), F32),
            pltpu.VMEM((1, D), F32),
            pltpu.VMEM((1, D), F32),
            pltpu.VMEM((8, 1152), jnp.int32),
            pltpu.VMEM((720, 128), jnp.int32),
            pltpu.VMEM((16, 256), F32),
            pltpu.VMEM((112, D), BF),
            pltpu.VMEM((112, D), BF),
            pltpu.SemaphoreType.DMA((COPIES,)),
            pltpu.SemaphoreType.DMA((COPIES,)),
            pltpu.SemaphoreType.DMA((20,)),
        ],
        compiler_params=pltpu.CompilerParams(
            collective_id=0, has_side_effects=True, vmem_limit_bytes=64 << 20
        ),
    )(
        shifts,
        fine_scale,
        coarse_scale,
        tokens.reshape(rows * columns, width),
        fine_qkv,
        fine_out,
        merge_weight,
        coarse_qkv,
        coarse_out,
        fine_table.T,
        coarse_table.T,
        bias_index,
        fine_gain.reshape(1, -1),
        merge_gain.reshape(1, -1),
        coarse_gain.reshape(1, -1),
        jnp.asarray(by_row),
        jnp.asarray(by_column),
    )
    return result.reshape(rows, columns, width)


def solution(mesh):
    placed = (
        P("lat", "lon", None),
        P("lat", None),
        P("lat", None),
        P(),
        P(),
        P(),
        P("lat", None),
        P(),
        P("lat", None),
        P("lat", None),
        P(),
        P(),
        P(),
        P(),
        P(),
    )
    return jax.shard_map(
        per_device, mesh=mesh, in_specs=placed, out_specs=P("lat", "lon", None), check_vma=False
    )
```

```python
import functools

import jax
import jax.numpy as jnp
import numpy as np
from jax import lax
from jax.experimental import pallas as pl
from jax.experimental.pallas import tpu as pltpu
from jax.sharding import PartitionSpec as P

MESH = pl.DeviceIdType.MESH
HEADS = 8
WLAT = 6
WLON = 12
WIN = 72
PAD = 80
D = 512
BF = jnp.bfloat16
F32 = jnp.float32

ABOVE, BELOW, OWN, LEFT, RIGHT, ABOVE_C, BELOW_C = 0, 128, 256, 544, 688, 832, 944
POOL = 1056
C_LEFT, C_RIGHT, C_ABOVE, C_BELOW, C_ABOVE_C, C_BELOW_C = 80, 160, 240, 320, 400, 512
CPOOL = 624
FINE_WINDOWS = [(0, 1), (1, 1), (2, 1), (1, 0), (1, 2), (0, 0), (0, 2), (2, 0), (2, 2)]
COARSE_WINDOWS = [(0, 0), (0, 1), (1, 0), (1, 1)]
LOG2E = 1.4426950408889634
NOWHERE = -200000
UNUSED = -100000


def code(row, column):
    return (row + 32) * 128 + column + 32


def padded_codes(places, length, fill):
    out = np.full((length,), fill, np.int32)
    out[: len(places)] = [code(r, c) for r, c in places]
    return out


def grid_places(rows, columns):
    return [(r, c) for r in rows for c in columns]


def frame_places(windows):
    parts = []
    for a, b in windows:
        rows = range(WLAT * a - WLAT, WLAT * a)
        columns = range(WLON * b - WLON, WLON * b)
        parts.append(grid_places(rows, columns))
    return parts


def blocks_of(parts, block, fill):
    return np.concatenate([padded_codes(p, block, fill) for p in parts])


def code_tables():
    own = grid_places(range(12), range(24))
    far_left = grid_places(range(12), range(-11, 0))
    far_right = grid_places(range(12), range(24, 35))
    sides = list(range(-11, 0)) + list(range(24, 35))
    above, below = range(-5, 0), range(12, 17)
    pool = np.concatenate(
        [
            padded_codes(grid_places(above, range(24)), 128, NOWHERE),
            padded_codes(grid_places(below, range(24)), 128, NOWHERE),
            padded_codes(own, 288, NOWHERE),
            padded_codes(far_left, 144, NOWHERE),
            padded_codes(far_right, 144, NOWHERE),
            padded_codes(grid_places(above, sides), 112, NOWHERE),
            padded_codes(grid_places(below, sides), 112, NOWHERE),
        ]
    )
    quads = [
        [(2 * a + i, 2 * b + j) for a in range(6) for b in range(12)]
        for j in range(2)
        for i in range(2)
    ]
    coarse_sides = list(range(-11, 0)) + list(range(12, 23))
    coarse_tiles = [(0, 0), (0, -1), (0, 1), (-1, 0), (1, 0)]
    coarse_pool = np.concatenate(
        [
            padded_codes(
                grid_places(range(6 * i, 6 * i + 6), range(12 * j, 12 * j + 12)), PAD, NOWHERE
            )
            for i, j in coarse_tiles
        ]
        + [
            padded_codes(grid_places(range(-5, 0), coarse_sides), 112, NOWHERE),
            padded_codes(grid_places(range(6, 11), coarse_sides), 112, NOWHERE),
        ]
    )
    fine_frame, coarse_frame = frame_places(FINE_WINDOWS), frame_places(COARSE_WINDOWS)
    by_row = np.full((8, 1152), NOWHERE, np.int32)
    for at, values in enumerate(
        [
            pool,
            blocks_of(fine_frame, PAD, NOWHERE),
            blocks_of(quads, PAD, NOWHERE),
            coarse_pool,
            blocks_of(coarse_frame, PAD, NOWHERE),
        ]
    ):
        by_row[at, : len(values)] = values
    by_column = np.full((720, 128), UNUSED, np.int32)
    for at, values in enumerate(
        [
            blocks_of(fine_frame, PAD, UNUSED),
            blocks_of(quads, PAD, UNUSED),
            blocks_of(coarse_frame, PAD, UNUSED),
            blocks_of([grid_places(range(6), range(12))], PAD, UNUSED),
            padded_codes(own, 288, UNUSED),
            padded_codes(grid_places(range(12), range(13, 24)), 144, UNUSED),
            padded_codes(grid_places(range(12), range(11)), 144, UNUSED),
            padded_codes(grid_places(range(7, 12), range(24)), 128, UNUSED),
            padded_codes(grid_places(range(5), range(24)), 128, UNUSED),
            padded_codes(grid_places(range(7, 12), sides), 112, UNUSED),
            padded_codes(grid_places(range(5), sides), 112, UNUSED),
            padded_codes(grid_places(range(1, 6), coarse_sides), 112, UNUSED),
            padded_codes(grid_places(range(5), coarse_sides), 112, UNUSED),
        ]
    ):
        by_column[: len(values), at] = values
    return by_row, by_column


def norm_rows(values, gain):
    middle = jnp.mean(values, axis=-1, keepdims=True)
    centered = values - middle
    spread = jnp.mean(centered * centered, axis=-1, keepdims=True)
    return centered * lax.rsqrt(spread + 1e-05) * gain


def dot(a, b):
    return jnp.dot(a, b, preferred_element_type=F32)


def dot_nt(a, b):
    return lax.dot_general(a, b, (((1,), (1,)), ((), ())), preferred_element_type=F32)


def kernel(
    shifts,
    fine_scale,
    coarse_scale,
    hbm_tokens,
    w_fine_qkv,
    w_fine_out,
    w_merge,
    w_coarse_qkv,
    w_coarse_out,
    hbm_fine_table,
    hbm_coarse_table,
    hbm_bias_index,
    hbm_fine_gain,
    hbm_merge_gain,
    hbm_coarse_gain,
    hbm_by_row,
    hbm_by_column,
    out,
    fine_qkv,
    fine_out,
    merge,
    coarse_qkv,
    coarse_out,
    pool,
    to_right,
    to_left,
    to_below,
    to_above,
    to_below_c,
    to_above_c,
    query,
    key,
    value,
    mixed,
    fine_after,
    coarse_pool,
    bias,
    tokens,
    fine_table,
    coarse_table,
    bias_index,
    fine_gain,
    merge_gain,
    coarse_gain,
    by_row,
    by_column,
    tables,
    to_below_k,
    to_above_k,
    send_sem,
    recv_sem,
    local_sem,
):
    lat, lon = lax.axis_index("lat"), lax.axis_index("lon")
    core, z_lo = lat % 2, lat // 2
    x, z_hi, y = lon // 8, (lon // 4) % 2, lon % 4
    z = z_hi * 8 + z_lo

    def place(x, y, z, core):
        x, y, z = (x + 4) % 4, (y + 4) % 4, (z + 16) % 16
        return ((z % 8) * 2 + core, x * 8 + (z // 8) * 4 + y)

    def along_z(d):
        return place(x, y, z + d, core)

    def along_x(d):
        return place(x + d, y, z, core)

    def along_y(d):
        return place(x, y + d, z, core)

    line = z * 2 + core

    def along_lat(d):
        spot = (line + d + 32) % 32
        return place(x, y, spot // 2, spot % 2)

    def along_lon(d):
        return (lat, (lon + d + 32) % 32)

    sibling = place(x, y, z, 1 - core)
    opposite = 4 - 8 * core
    hops = (opposite, 3, -3, 2, -2, 1, -1)

    barrier = pltpu.get_barrier_semaphore()
    senders = [along_z(-d) for d in hops]
    senders += [along_x(d) for d in (1, -1, 2)] + [along_y(d) for d in (1, -1, 2)]
    senders += [sibling, along_lon(1), along_lon(-1), along_lat(1), along_lat(-1)]
    for device in senders:
        pl.semaphore_signal(barrier, inc=1, device_id=device, device_id_type=MESH)

    local_count = [0]

    def bring(source, target):
        at = local_count[0]
        local_count[0] += 1
        copy = pltpu.make_async_copy(source, target, local_sem.at[at])
        copy.start()
        return copy

    first = [
        bring(hbm_tokens, tokens),
        bring(hbm_by_row, by_row),
        bring(hbm_by_column, by_column),
    ]
    later = [
        bring(hbm_fine_table, fine_table),
        bring(hbm_coarse_table, coarse_table),
        bring(hbm_bias_index, bias_index),
        bring(hbm_fine_gain, fine_gain),
        bring(hbm_merge_gain, merge_gain),
        bring(hbm_coarse_gain, coarse_gain),
    ]

    def picked(column, rows, row_at, first, width, offset=0):
        left = by_column[0:rows, column : column + 1] + offset
        right = by_row[row_at : row_at + 1, first : first + width]
        return jnp.where(left == right, 1.0, 0.0).astype(BF)

    counter = [0]
    sent = []

    def send(source, target, device):
        at = counter[0]
        counter[0] += 1
        copy = pltpu.make_async_remote_copy(
            src_ref=source,
            dst_ref=target,
            send_sem=send_sem.at[at],
            recv_sem=recv_sem.at[at],
            device_id=device,
            device_id_type=MESH,
        )
        copy.start()
        sent.append(copy)
        return copy

    def arrived(copies):
        for copy in copies:
            copy.wait_recv()

    class Gather:
        def __init__(self, shard, whole, halves):
            self.shard, self.whole, self.halves = shard, whole, halves

        def start(self):
            self.ready, self.waits = [], []
            for axis, part, pair_axis, small in self.halves:
                rows, columns = small
                source = self.shard.at[rows, columns]
                target = self.whole.at[z_lo, core, rows, columns]
                self.ready.append(bring(source, target))
                for d in hops:
                    self.waits.append(send(source, target, along_z(d)))

        def begun(self):
            for copy in self.ready:
                copy.wait()
            arrived(self.waits)
            self.ready, self.waits = [], []

        def pair(self):
            self.begun()
            for axis, part, pair_axis, (rows, columns) in self.halves:
                area = self.whole.at[:, core, rows, columns]
                self.waits.append(send(area, area, pair_axis(1)))

        def spread(self):
            self.begun()
            for axis, (rows, columns), pair_axis, small in self.halves:
                area = self.whole.at[:, core, rows, columns]
                for d in (1, -1, 2):
                    self.waits.append(send(area, area, axis(d)))

        def share(self):
            arrived(self.waits)
            part = self.whole.at[:, core]
            self.waits = [send(part, part, sibling)]

        def finish(self):
            arrived(self.waits)

    def by_x(part):
        return along_x, part(x), along_y, part(x, y % 2)

    def by_y(part):
        return along_y, part(y), along_x, part(y, x % 2)

    def corner(first, width):
        def part(g, half=None):
            rows = pl.ds(pl.multiple_of((g // 2) * 16, 16), 16)
            at, wide = first + (g % 2) * width, width
            if half is not None:
                at, wide = at + half * (width // 2), width // 2
            return rows, pl.ds(pl.multiple_of(at, 128), wide)

        return part

    def band(first, width):
        def part(g, half=None):
            if half is None:
                return pl.ds(pl.multiple_of(g * 32, 32), 32), pl.ds(first, width)
            return pl.ds(pl.multiple_of(g * 32 + half * 16, 16), 16), pl.ds(first, width)

        return part

    def quarters(axis, g, first):
        part = corner(first, 384)(g)
        return axis, part, None, part

    g_fine_qkv = Gather(
        w_fine_qkv, fine_qkv, [quarters(along_x, x, 0), quarters(along_y, y, 768)]
    )
    g_fine_out = Gather(w_fine_out, fine_out, [by_x(corner(0, 256))])
    g_merge = Gather(w_merge, merge, [by_x(band(0, 256)), by_y(band(256, 256))])
    g_coarse_qkv = Gather(w_coarse_qkv, coarse_qkv, [by_x(corner(0, 768))])
    g_coarse_out = Gather(w_coarse_out, coarse_out, [by_y(corner(0, 256))])

    pl.semaphore_wait(barrier, len(senders))
    g_fine_qkv.start()
    g_fine_out.start()
    g_merge.start()
    for copy in first:
        copy.wait()
    own = tokens[...]
    to_right[...] = dot(picked(5, 144, 0, OWN, 288), own).astype(BF)
    to_left[...] = dot(picked(6, 144, 0, OWN, 288), own).astype(BF)
    to_below[...] = dot(picked(7, 128, 0, OWN, 288), own).astype(BF)
    to_above[...] = dot(picked(8, 128, 0, OWN, 288), own).astype(BF)
    pool[OWN : OWN + 288, :] = own

    g_fine_qkv.spread()
    side_copies = [
        send(to_right, pool.at[pl.ds(LEFT, 144)], along_lon(1)),
        send(to_left, pool.at[pl.ds(RIGHT, 144)], along_lon(-1)),
    ]
    row_copies = [
        send(to_below, pool.at[pl.ds(ABOVE, 128)], along_lat(1)),
        send(to_above, pool.at[pl.ds(BELOW, 128)], along_lat(-1)),
    ]
    bias[...] = jnp.zeros((16, PAD, 128), F32)
    tables[...] = jnp.zeros((16, 256), F32)
    for copy in later:
        copy.wait()
    tables[0:HEADS, 0:253] = fine_table[...]
    tables[HEADS : 2 * HEADS, 0:253] = coarse_table[...]
    table = tables[...]
    top = table.astype(BF)
    rest = table - top.astype(F32)
    middle = rest.astype(BF)
    bottom = (rest - middle.astype(F32)).astype(BF)
    table_parts = jnp.concatenate([top, middle, bottom], axis=0)
    levels = lax.broadcasted_iota(jnp.int32, (256, WIN), 0)

    def bias_rows(group, carry):
        rows = bias_index[pl.ds(pl.multiple_of(group * 8, 8), 8), :]
        for i in range(8):
            hot = jnp.where(levels == rows[i : i + 1, :], 1.0, 0.0).astype(BF)
            parts = dot(table_parts, hot)
            looked = (parts[0:16] + parts[16:32] + parts[32:48]) * LOG2E
            bias[:, pl.ds(group * 8 + i, 1), 0:WIN] = looked.reshape(16, 1, WIN)
        return carry

    lax.fori_loop(0, WIN // 8, bias_rows, 0)

    g_fine_qkv.share()
    g_fine_out.pair()
    g_merge.pair()

    lane = lax.broadcasted_iota(jnp.int32, (1, 128), 1)
    low = jnp.where(lane < 64, 1.0, 0.0).astype(BF)
    high = jnp.where(lane < 64, 0.0, 1.0).astype(BF)
    position = lax.broadcasted_iota(jnp.int32, (PAD, 128), 0)
    row_of = jnp.zeros((PAD, 128), jnp.int32)
    for r in range(1, WLAT):
        row_of = row_of + jnp.where(position >= WLON * r, 1, 0)
    ones_row = lax.broadcasted_iota(jnp.int32, (256, 256), 0) // 64
    ones_column = lax.broadcasted_iota(jnp.int32, (256, 256), 1) // 64
    same_head = jnp.where(ones_row == ones_column, 1.0, 0.0).astype(BF)

    def scale_row(scale):
        head_of = lax.broadcasted_iota(jnp.int32, (1, D), 1) // 64
        row = jnp.zeros((1, D), F32)
        for n in range(HEADS):
            row = jnp.where(head_of == n, scale[n] * LOG2E, row)
        return row

    def framed(level, windows, column, row_at, cells, first, width):
        offset = shifts[level, 0] * 128 + shifts[level, 1]
        at, count = windows
        left = by_column[at * PAD : (at + count) * PAD, column : column + 1] + offset
        right = by_row[row_at : row_at + 1, first : first + width]
        hot = jnp.where(left == right, 1.0, 0.0).astype(BF)
        return dot(hot, cells[first : first + width, :])

    def project(windows, cells, weights, scale):
        scales = scale_row(scale)
        at, count = windows
        frame = cells.astype(BF)
        for n in range(6):
            block = weights[:, :, :, 256 * n : 256 * n + 256].reshape(D, 256)
            rounded = dot(frame, block).astype(BF)
            columns = slice(256 * (n % 2), 256 * (n % 2) + 256)
            if n < 4:
                full = rounded.astype(F32)
                square = dot((full * full).astype(BF), same_head)
                full = full * lax.rsqrt(square + 1e-06)
                if n < 2:
                    full = full * scales[:, columns]
                rounded = full.astype(BF)
            target = (query, key, value)[n // 2]
            target[at : at + count, :, columns] = rounded.reshape(count, PAD, 256)

    def attend(level, windows, row_block, rows_here):
        first_row = lat * rows_here + shifts[level, 0] - WLAT
        at, count = windows

        def one(w, carry):
            latitude = row_of + (first_row + WLAT * row_block(w))
            here = (latitude >= 0) & (latitude < rows_here * 16) & (position < WIN)
            keep = jnp.where(here, 1.0, 0.0).astype(BF)
            for p in range(HEADS // 2):
                columns = slice(128 * p, 128 * p + 128)
                q = query[at + w, :, columns]
                pair = jnp.concatenate([q * low, q * high], axis=0)
                scores = dot_nt(pair, key[at + w, :, columns])
                own_bias = bias[8 * level + 2 * p : 8 * level + 2 * p + 2, :, 0:PAD]
                powers = jnp.exp2(scores + own_bias.reshape(2 * PAD, PAD)).astype(BF)
                kept = jnp.concatenate([value[at + w, :, columns] * keep, keep], axis=1)
                both = dot(powers, kept)
                mine = jnp.where(lane < 64, both[0:PAD, 0:128], both[PAD : 2 * PAD, 0:128])
                total = jnp.where(lane < 64, both[0:PAD, 128:256], both[PAD : 2 * PAD, 128:256])
                taken = mine / total
                mixed[at + w, :, columns] = taken.astype(BF)
            return carry

        lax.fori_loop(0, count, one, 0, unroll=True)

    def finish(level, windows, column, rows, row_at, weights, base, gain):
        offset = shifts[level, 0] * 128 + shifts[level, 1]
        left = by_column[0:rows, column : column + 1] - offset
        right = by_row[row_at : row_at + 1, 0 : windows * PAD]
        hot = jnp.where(left == right, 1.0, 0.0).astype(BF)
        taken = dot(hot, mixed[0:windows].reshape(windows * PAD, D)).astype(BF)
        branch = dot(taken, weights[...].reshape(D, D))
        return (base + norm_rows(branch, gain)).astype(BF)

    g_fine_qkv.finish()
    arrived(row_copies)
    frame = framed(0, (0, 3), 0, 0, pool, ABOVE, 544)
    project((0, 3), frame, fine_qkv, fine_scale)
    g_fine_out.spread()
    g_merge.spread()
    attend(0, (0, 3), lambda w: w, 12)

    arrived(side_copies)
    near = pool[OWN : OWN + 576, :]
    to_below_c[...] = dot(picked(9, 112, 0, OWN, 576), near).astype(BF)
    to_above_c[...] = dot(picked(10, 112, 0, OWN, 576), near).astype(BF)
    row_copies = [
        send(to_below_c, pool.at[pl.ds(ABOVE_C, 112)], along_lat(1)),
        send(to_above_c, pool.at[pl.ds(BELOW_C, 112)], along_lat(-1)),
    ]
    g_coarse_qkv.start()
    g_coarse_out.start()
    frame = framed(0, (3, 2), 0, 0, pool, OWN, 576)
    project((3, 2), frame, fine_qkv, fine_scale)
    attend(0, (3, 2), lambda w: 1, 12)

    frame = framed(0, (5, 4), 0, 0, pool, 0, ABOVE_C)
    arrived(row_copies)
    frame = frame + framed(0, (5, 4), 0, 0, pool, ABOVE_C, POOL - ABOVE_C)
    project((5, 4), frame, fine_qkv, fine_scale)
    g_fine_out.share()
    attend(0, (5, 4), lambda w: 2 * (w // 2), 12)
    g_merge.share()
    g_fine_out.finish()
    in_quads = dot(picked(1, 320, 0, OWN, 288), tokens[...])
    fine_after[...] = finish(0, 9, 1, 320, 1, fine_out, in_quads, fine_gain[...])
    g_coarse_qkv.pair()
    g_coarse_out.pair()
    g_merge.finish()
    merged = jnp.zeros((PAD, D), F32)
    for p in range(4):
        rows = merge[2 * p : 2 * p + 2].reshape(D, D)
        merged = merged + dot(fine_after[PAD * p : PAD * p + PAD, :], rows)
    coarse_pool[0:PAD, :] = norm_rows(merged, merge_gain[...]).astype(BF)
    mine = coarse_pool.at[pl.ds(0, PAD)]
    side_copies = [
        send(mine, coarse_pool.at[pl.ds(C_LEFT, PAD)], along_lon(1)),
        send(mine, coarse_pool.at[pl.ds(C_RIGHT, PAD)], along_lon(-1)),
    ]
    row_copies = [
        send(mine, coarse_pool.at[pl.ds(C_ABOVE, PAD)], along_lat(1)),
        send(mine, coarse_pool.at[pl.ds(C_BELOW, PAD)], along_lat(-1)),
    ]
    g_coarse_qkv.spread()
    g_coarse_out.spread()
    arrived(side_copies)
    near = coarse_pool[0 : 3 * PAD, :]
    to_below_k[...] = dot(picked(11, 112, 3, 0, 3 * PAD), near).astype(BF)
    to_above_k[...] = dot(picked(12, 112, 3, 0, 3 * PAD), near).astype(BF)
    row_copies += [
        send(to_below_k, coarse_pool.at[pl.ds(C_ABOVE_C, 112)], along_lat(1)),
        send(to_above_k, coarse_pool.at[pl.ds(C_BELOW_C, 112)], along_lat(-1)),
    ]
    g_coarse_qkv.share()
    g_coarse_out.share()
    frame = framed(1, (0, 4), 2, 3, coarse_pool, 0, C_ABOVE)
    g_coarse_qkv.finish()
    arrived(row_copies[:2])
    frame = frame + framed(1, (0, 4), 2, 3, coarse_pool, C_ABOVE, C_ABOVE_C - C_ABOVE)
    arrived(row_copies[2:])
    corners = CPOOL - C_ABOVE_C
    frame = frame + framed(1, (0, 4), 2, 3, coarse_pool, C_ABOVE_C, corners)
    project((0, 4), frame, coarse_qkv, coarse_scale)
    attend(1, (0, 4), lambda w: w // 2, 6)
    g_coarse_out.finish()
    base = coarse_pool[0:PAD, :].astype(F32)
    coarse_after = finish(1, 4, 3, PAD, 4, coarse_out, base, coarse_gain[...]).astype(F32)
    for p in range(4):
        part = fine_after[PAD * p : PAD * p + PAD, :].astype(F32) + coarse_after
        fine_after[PAD * p : PAD * p + PAD, :] = part.astype(BF)
    out[...] = dot(picked(4, 288, 2, 0, 320), fine_after[...]).astype(BF)
    for copy in sent:
        copy.wait_send()


COPIES = 12 + 21 + 12 + 23 + 12 + 12


def per_device(
    tokens,
    fine_qkv,
    fine_out,
    fine_scale,
    fine_table,
    fine_gain,
    merge_weight,
    merge_gain,
    coarse_qkv,
    coarse_out,
    coarse_scale,
    coarse_table,
    coarse_gain,
    shifts,
    bias_index,
):
    by_row, by_column = code_tables()
    rows, columns, width = tokens.shape
    smem = pl.BlockSpec(memory_space=pltpu.SMEM)
    vmem = pl.BlockSpec(memory_space=pltpu.VMEM)
    hbm = pl.BlockSpec(memory_space=pltpu.HBM)
    result = pl.pallas_call(
        kernel,
        out_shape=jax.ShapeDtypeStruct((rows * columns, width), BF),
        in_specs=[smem] * 3 + [hbm] * 14,
        out_specs=vmem,
        scratch_shapes=[
            pltpu.VMEM((8, 2, 32, 1536), BF),
            pltpu.VMEM((8, 2, 32, 512), BF),
            pltpu.VMEM((8, 2, 128, 512), BF),
            pltpu.VMEM((8, 2, 32, 1536), BF),
            pltpu.VMEM((8, 2, 32, 512), BF),
            pltpu.VMEM((POOL, D), BF),
            pltpu.VMEM((144, D), BF),
            pltpu.VMEM((144, D), BF),
            pltpu.VMEM((128, D), BF),
            pltpu.VMEM((128, D), BF),
            pltpu.VMEM((112, D), BF),
            pltpu.VMEM((112, D), BF),
            pltpu.VMEM((9, PAD, D), BF),
            pltpu.VMEM((9, PAD, D), BF),
            pltpu.VMEM((9, PAD, D), BF),
            pltpu.VMEM((9, PAD, D), BF),
            pltpu.VMEM((320, D), BF),
            pltpu.VMEM((CPOOL, D), BF),
            pltpu.VMEM((16, PAD, 128), F32),
            pltpu.VMEM((288, D), BF),
            pltpu.VMEM((HEADS, 253), F32),
            pltpu.VMEM((HEADS, 253), F32),
            pltpu.VMEM((WIN, WIN), jnp.int32),
            pltpu.VMEM((1, D), F32),
            pltpu.VMEM((1, D), F32),
            pltpu.VMEM((1, D), F32),
            pltpu.VMEM((8, 1152), jnp.int32),
            pltpu.VMEM((720, 128), jnp.int32),
            pltpu.VMEM((16, 256), F32),
            pltpu.VMEM((112, D), BF),
            pltpu.VMEM((112, D), BF),
            pltpu.SemaphoreType.DMA((COPIES,)),
            pltpu.SemaphoreType.DMA((COPIES,)),
            pltpu.SemaphoreType.DMA((20,)),
        ],
        compiler_params=pltpu.CompilerParams(
            collective_id=0, has_side_effects=True, vmem_limit_bytes=64 << 20
        ),
    )(
        shifts,
        fine_scale,
        coarse_scale,
        tokens.reshape(rows * columns, width),
        fine_qkv,
        fine_out,
        merge_weight,
        coarse_qkv,
        coarse_out,
        fine_table.T,
        coarse_table.T,
        bias_index,
        fine_gain.reshape(1, -1),
        merge_gain.reshape(1, -1),
        coarse_gain.reshape(1, -1),
        jnp.asarray(by_row),
        jnp.asarray(by_column),
    )
    return result.reshape(rows, columns, width)


def solution(mesh):
    placed = (
        P("lat", "lon", None),
        P("lat", None),
        P("lat", None),
        P(),
        P(),
        P(),
        P("lat", None),
        P(),
        P("lat", None),
        P("lat", None),
        P(),
        P(),
        P(),
        P(),
        P(),
    )
    return jax.shard_map(
        per_device, mesh=mesh, in_specs=placed, out_specs=P("lat", "lon", None), check_vma=False
    )
```

```python
import functools

import jax
import jax.numpy as jnp
import numpy as np
from jax import lax
from jax.experimental import pallas as pl
from jax.experimental.pallas import tpu as pltpu
from jax.sharding import PartitionSpec as P

MESH = pl.DeviceIdType.MESH
HEADS = 8
WLAT = 6
WLON = 12
WIN = 72
PAD = 80
D = 512
BF = jnp.bfloat16
F32 = jnp.float32

ABOVE, BELOW, OWN, LEFT, RIGHT, ABOVE_C, BELOW_C = 0, 128, 256, 544, 688, 832, 944
POOL = 1056
C_LEFT, C_RIGHT, C_ABOVE, C_BELOW, C_ABOVE_C, C_BELOW_C = 80, 160, 240, 320, 400, 512
CPOOL = 624
FINE_WINDOWS = [(0, 1), (1, 1), (2, 1), (1, 0), (1, 2), (0, 0), (0, 2), (2, 0), (2, 2)]
COARSE_WINDOWS = [(0, 0), (0, 1), (1, 0), (1, 1)]
LOG2E = 1.4426950408889634
NOWHERE = -200000
UNUSED = -100000


def code(row, column):
    return (row + 32) * 128 + column + 32


def padded_codes(places, length, fill):
    out = np.full((length,), fill, np.int32)
    out[: len(places)] = [code(r, c) for r, c in places]
    return out


def grid_places(rows, columns):
    return [(r, c) for r in rows for c in columns]


def frame_places(windows):
    parts = []
    for a, b in windows:
        rows = range(WLAT * a - WLAT, WLAT * a)
        columns = range(WLON * b - WLON, WLON * b)
        parts.append(grid_places(rows, columns))
    return parts


def blocks_of(parts, block, fill):
    return np.concatenate([padded_codes(p, block, fill) for p in parts])


def code_tables():
    own = grid_places(range(12), range(24))
    far_left = grid_places(range(12), range(-11, 0))
    far_right = grid_places(range(12), range(24, 35))
    sides = list(range(-11, 0)) + list(range(24, 35))
    above, below = range(-5, 0), range(12, 17)
    pool = np.concatenate(
        [
            padded_codes(grid_places(above, range(24)), 128, NOWHERE),
            padded_codes(grid_places(below, range(24)), 128, NOWHERE),
            padded_codes(own, 288, NOWHERE),
            padded_codes(far_left, 144, NOWHERE),
            padded_codes(far_right, 144, NOWHERE),
            padded_codes(grid_places(above, sides), 112, NOWHERE),
            padded_codes(grid_places(below, sides), 112, NOWHERE),
        ]
    )
    quads = [
        [(2 * a + i, 2 * b + j) for a in range(6) for b in range(12)]
        for j in range(2)
        for i in range(2)
    ]
    coarse_sides = list(range(-11, 0)) + list(range(12, 23))
    coarse_tiles = [(0, 0), (0, -1), (0, 1), (-1, 0), (1, 0)]
    coarse_pool = np.concatenate(
        [
            padded_codes(
                grid_places(range(6 * i, 6 * i + 6), range(12 * j, 12 * j + 12)), PAD, NOWHERE
            )
            for i, j in coarse_tiles
        ]
        + [
            padded_codes(grid_places(range(-5, 0), coarse_sides), 112, NOWHERE),
            padded_codes(grid_places(range(6, 11), coarse_sides), 112, NOWHERE),
        ]
    )
    fine_frame, coarse_frame = frame_places(FINE_WINDOWS), frame_places(COARSE_WINDOWS)
    by_row = np.full((8, 1152), NOWHERE, np.int32)
    for at, values in enumerate(
        [
            pool,
            blocks_of(fine_frame, PAD, NOWHERE),
            blocks_of(quads, PAD, NOWHERE),
            coarse_pool,
            blocks_of(coarse_frame, PAD, NOWHERE),
        ]
    ):
        by_row[at, : len(values)] = values
    by_column = np.full((720, 128), UNUSED, np.int32)
    for at, values in enumerate(
        [
            blocks_of(fine_frame, PAD, UNUSED),
            blocks_of(quads, PAD, UNUSED),
            blocks_of(coarse_frame, PAD, UNUSED),
            blocks_of([grid_places(range(6), range(12))], PAD, UNUSED),
            padded_codes(own, 288, UNUSED),
            padded_codes(grid_places(range(12), range(13, 24)), 144, UNUSED),
            padded_codes(grid_places(range(12), range(11)), 144, UNUSED),
            padded_codes(grid_places(range(7, 12), range(24)), 128, UNUSED),
            padded_codes(grid_places(range(5), range(24)), 128, UNUSED),
            padded_codes(grid_places(range(7, 12), sides), 112, UNUSED),
            padded_codes(grid_places(range(5), sides), 112, UNUSED),
            padded_codes(grid_places(range(1, 6), coarse_sides), 112, UNUSED),
            padded_codes(grid_places(range(5), coarse_sides), 112, UNUSED),
        ]
    ):
        by_column[: len(values), at] = values
    return by_row, by_column


def norm_rows(values, gain):
    middle = jnp.mean(values, axis=-1, keepdims=True)
    centered = values - middle
    spread = jnp.mean(centered * centered, axis=-1, keepdims=True)
    return centered * lax.rsqrt(spread + 1e-05) * gain


def dot(a, b):
    return jnp.dot(a, b, preferred_element_type=F32)


def dot_nt(a, b):
    return lax.dot_general(a, b, (((1,), (1,)), ((), ())), preferred_element_type=F32)


def kernel(
    shifts,
    fine_scale,
    coarse_scale,
    hbm_tokens,
    w_fine_qkv,
    w_fine_out,
    w_merge,
    w_coarse_qkv,
    w_coarse_out,
    hbm_fine_table,
    hbm_coarse_table,
    hbm_bias_index,
    hbm_fine_gain,
    hbm_merge_gain,
    hbm_coarse_gain,
    hbm_by_row,
    hbm_by_column,
    out,
    fine_qkv,
    fine_out,
    merge,
    coarse_qkv,
    coarse_out,
    pool,
    to_right,
    to_left,
    to_below,
    to_above,
    to_below_c,
    to_above_c,
    query,
    key,
    value,
    mixed,
    fine_after,
    coarse_pool,
    bias,
    tokens,
    fine_table,
    coarse_table,
    bias_index,
    fine_gain,
    merge_gain,
    coarse_gain,
    by_row,
    by_column,
    tables,
    to_below_k,
    to_above_k,
    send_sem,
    recv_sem,
    local_sem,
):
    lat, lon = lax.axis_index("lat"), lax.axis_index("lon")
    core, z_lo = lat % 2, lat // 2
    x, z_hi, y = lon // 8, (lon // 4) % 2, lon % 4
    z = z_hi * 8 + z_lo

    def place(x, y, z, core):
        x, y, z = (x + 4) % 4, (y + 4) % 4, (z + 16) % 16
        return ((z % 8) * 2 + core, x * 8 + (z // 8) * 4 + y)

    def along_z(d):
        return place(x, y, z + d, core)

    def along_x(d):
        return place(x + d, y, z, core)

    def along_y(d):
        return place(x, y + d, z, core)

    line = z * 2 + core

    def along_lat(d):
        spot = (line + d + 32) % 32
        return place(x, y, spot // 2, spot % 2)

    def along_lon(d):
        return (lat, (lon + d + 32) % 32)

    sibling = place(x, y, z, 1 - core)
    opposite = 4 - 8 * core
    hops = (opposite, 3, -3, 2, -2, 1, -1)

    barrier = pltpu.get_barrier_semaphore()
    senders = [along_z(-d) for d in hops]
    senders += [along_x(d) for d in (1, -1, 2)] + [along_y(d) for d in (1, -1, 2)]
    senders += [sibling, along_lon(1), along_lon(-1), along_lat(1), along_lat(-1)]
    for device in senders:
        pl.semaphore_signal(barrier, inc=1, device_id=device, device_id_type=MESH)

    local_count = [0]

    def bring(source, target):
        at = local_count[0]
        local_count[0] += 1
        copy = pltpu.make_async_copy(source, target, local_sem.at[at])
        copy.start()
        return copy

    first = [
        bring(hbm_tokens, tokens),
        bring(hbm_by_row, by_row),
        bring(hbm_by_column, by_column),
    ]
    later = [
        bring(hbm_fine_table, fine_table),
        bring(hbm_coarse_table, coarse_table),
        bring(hbm_bias_index, bias_index),
        bring(hbm_fine_gain, fine_gain),
        bring(hbm_merge_gain, merge_gain),
        bring(hbm_coarse_gain, coarse_gain),
    ]

    def picked(column, rows, row_at, first, width, offset=0):
        left = by_column[0:rows, column : column + 1] + offset
        right = by_row[row_at : row_at + 1, first : first + width]
        return jnp.where(left == right, 1.0, 0.0).astype(BF)

    counter = [0]
    sent = []

    def send(source, target, device):
        at = counter[0]
        counter[0] += 1
        copy = pltpu.make_async_remote_copy(
            src_ref=source,
            dst_ref=target,
            send_sem=send_sem.at[at],
            recv_sem=recv_sem.at[at],
            device_id=device,
            device_id_type=MESH,
        )
        copy.start()
        sent.append(copy)
        return copy

    def arrived(copies):
        for copy in copies:
            copy.wait_recv()

    class Gather:
        def __init__(self, shard, whole, halves):
            self.shard, self.whole, self.halves = shard, whole, halves

        def start(self):
            self.ready, self.waits = [], []
            for axis, part, pair_axis, small in self.halves:
                rows, columns = small
                source = self.shard.at[rows, columns]
                target = self.whole.at[z_lo, core, rows, columns]
                self.ready.append(bring(source, target))
                for d in hops:
                    self.waits.append(send(source, target, along_z(d)))

        def begun(self):
            for copy in self.ready:
                copy.wait()
            arrived(self.waits)
            self.ready, self.waits = [], []

        def pair(self):
            self.begun()
            for axis, part, pair_axis, (rows, columns) in self.halves:
                area = self.whole.at[:, core, rows, columns]
                self.waits.append(send(area, area, pair_axis(1)))

        def spread(self):
            self.begun()
            for axis, (rows, columns), pair_axis, small in self.halves:
                area = self.whole.at[:, core, rows, columns]
                for d in (1, -1, 2):
                    self.waits.append(send(area, area, axis(d)))

        def share(self):
            arrived(self.waits)
            part = self.whole.at[:, core]
            self.waits = [send(part, part, sibling)]

        def finish(self):
            arrived(self.waits)

    def by_x(part):
        return along_x, part(x), along_y, part(x, y % 2)

    def by_y(part):
        return along_y, part(y), along_x, part(y, x % 2)

    def corner(first, width):
        def part(g, half=None):
            rows = pl.ds(pl.multiple_of((g // 2) * 16, 16), 16)
            at, wide = first + (g % 2) * width, width
            if half is not None:
                at, wide = at + half * (width // 2), width // 2
            return rows, pl.ds(pl.multiple_of(at, 128), wide)

        return part

    def band(first, width):
        def part(g, half=None):
            if half is None:
                return pl.ds(pl.multiple_of(g * 32, 32), 32), pl.ds(first, width)
            return pl.ds(pl.multiple_of(g * 32 + half * 16, 16), 16), pl.ds(first, width)

        return part

    def quarters(axis, g, first):
        part = corner(first, 384)(g)
        return axis, part, None, part

    g_fine_qkv = Gather(
        w_fine_qkv, fine_qkv, [quarters(along_x, x, 0), quarters(along_y, y, 768)]
    )
    g_fine_out = Gather(w_fine_out, fine_out, [by_x(corner(0, 256))])
    g_merge = Gather(w_merge, merge, [by_x(band(0, 256)), by_y(band(256, 256))])
    g_coarse_qkv = Gather(w_coarse_qkv, coarse_qkv, [by_x(corner(0, 768))])
    g_coarse_out = Gather(w_coarse_out, coarse_out, [by_y(corner(0, 256))])

    pl.semaphore_wait(barrier, len(senders))
    g_fine_qkv.start()
    g_fine_out.start()
    g_merge.start()
    for copy in first:
        copy.wait()
    own = tokens[...]
    to_right[...] = dot(picked(5, 144, 0, OWN, 288), own).astype(BF)
    to_left[...] = dot(picked(6, 144, 0, OWN, 288), own).astype(BF)
    to_below[...] = dot(picked(7, 128, 0, OWN, 288), own).astype(BF)
    to_above[...] = dot(picked(8, 128, 0, OWN, 288), own).astype(BF)
    pool[OWN : OWN + 288, :] = own

    g_fine_qkv.spread()
    side_copies = [
        send(to_right, pool.at[pl.ds(LEFT, 144)], along_lon(1)),
        send(to_left, pool.at[pl.ds(RIGHT, 144)], along_lon(-1)),
    ]
    row_copies = [
        send(to_below, pool.at[pl.ds(ABOVE, 128)], along_lat(1)),
        send(to_above, pool.at[pl.ds(BELOW, 128)], along_lat(-1)),
    ]
    bias[...] = jnp.zeros((16, PAD, 128), F32)
    tables[...] = jnp.zeros((16, 256), F32)
    for copy in later:
        copy.wait()
    tables[0:HEADS, 0:253] = fine_table[...]
    tables[HEADS : 2 * HEADS, 0:253] = coarse_table[...]
    table = tables[...]
    top = table.astype(BF)
    rest = table - top.astype(F32)
    middle = rest.astype(BF)
    bottom = (rest - middle.astype(F32)).astype(BF)
    table_parts = jnp.concatenate([top, middle, bottom], axis=0)
    levels = lax.broadcasted_iota(jnp.int32, (256, WIN), 0)

    def bias_rows(group, carry):
        rows = bias_index[pl.ds(pl.multiple_of(group * 8, 8), 8), :]
        for i in range(8):
            hot = jnp.where(levels == rows[i : i + 1, :], 1.0, 0.0).astype(BF)
            parts = dot(table_parts, hot)
            looked = (parts[0:16] + parts[16:32] + parts[32:48]) * LOG2E
            bias[:, pl.ds(group * 8 + i, 1), 0:WIN] = looked.reshape(16, 1, WIN)
        return carry

    lax.fori_loop(0, WIN // 8, bias_rows, 0)

    g_fine_qkv.share()
    g_fine_out.pair()
    g_merge.pair()

    lane = lax.broadcasted_iota(jnp.int32, (1, 128), 1)
    low = jnp.where(lane < 64, 1.0, 0.0).astype(BF)
    high = jnp.where(lane < 64, 0.0, 1.0).astype(BF)
    position = lax.broadcasted_iota(jnp.int32, (PAD, 128), 0)
    row_of = jnp.zeros((PAD, 128), jnp.int32)
    for r in range(1, WLAT):
        row_of = row_of + jnp.where(position >= WLON * r, 1, 0)
    ones_row = lax.broadcasted_iota(jnp.int32, (256, 256), 0) // 64
    ones_column = lax.broadcasted_iota(jnp.int32, (256, 256), 1) // 64
    same_head = jnp.where(ones_row == ones_column, 1.0, 0.0).astype(BF)

    def scale_row(scale):
        head_of = lax.broadcasted_iota(jnp.int32, (1, D), 1) // 64
        row = jnp.zeros((1, D), F32)
        for n in range(HEADS):
            row = jnp.where(head_of == n, scale[n] * LOG2E, row)
        return row

    def framed(level, windows, column, row_at, cells, first, width):
        offset = shifts[level, 0] * 128 + shifts[level, 1]
        at, count = windows
        left = by_column[at * PAD : (at + count) * PAD, column : column + 1] + offset
        right = by_row[row_at : row_at + 1, first : first + width]
        hot = jnp.where(left == right, 1.0, 0.0).astype(BF)
        return dot(hot, cells[first : first + width, :])

    def project(windows, cells, weights, scale):
        scales = scale_row(scale)
        at, count = windows
        frame = cells.astype(BF)
        for n in range(6):
            block = weights[:, :, :, 256 * n : 256 * n + 256].reshape(D, 256)
            rounded = dot(frame, block).astype(BF)
            columns = slice(256 * (n % 2), 256 * (n % 2) + 256)
            if n < 4:
                full = rounded.astype(F32)
                square = dot((full * full).astype(BF), same_head)
                full = full * lax.rsqrt(square + 1e-06)
                if n < 2:
                    full = full * scales[:, columns]
                rounded = full.astype(BF)
            target = (query, key, value)[n // 2]
            target[at : at + count, :, columns] = rounded.reshape(count, PAD, 256)

    def attend(level, windows, row_block, rows_here):
        first_row = lat * rows_here + shifts[level, 0] - WLAT
        at, count = windows

        def one(w, carry):
            latitude = row_of + (first_row + WLAT * row_block(w))
            here = (latitude >= 0) & (latitude < rows_here * 16) & (position < WIN)
            keep = jnp.where(here, 1.0, 0.0).astype(BF)
            for p in range(HEADS // 2):
                columns = slice(128 * p, 128 * p + 128)
                q = query[at + w, :, columns]
                pair = jnp.concatenate([q * low, q * high], axis=0)
                scores = dot_nt(pair, key[at + w, :, columns])
                own_bias = bias[8 * level + 2 * p : 8 * level + 2 * p + 2, :, 0:PAD]
                powers = jnp.exp2(scores + own_bias.reshape(2 * PAD, PAD)).astype(BF)
                kept = jnp.concatenate([value[at + w, :, columns] * keep, keep], axis=1)
                both = dot(powers, kept)
                mine = jnp.where(lane < 64, both[0:PAD, 0:128], both[PAD : 2 * PAD, 0:128])
                total = jnp.where(lane < 64, both[0:PAD, 128:256], both[PAD : 2 * PAD, 128:256])
                taken = mine / total
                mixed[at + w, :, columns] = taken.astype(BF)
            return carry

        lax.fori_loop(0, count, one, 0, unroll=True)

    def finish(level, windows, column, rows, row_at, weights, base, gain):
        offset = shifts[level, 0] * 128 + shifts[level, 1]
        left = by_column[0:rows, column : column + 1] - offset
        right = by_row[row_at : row_at + 1, 0 : windows * PAD]
        hot = jnp.where(left == right, 1.0, 0.0).astype(BF)
        taken = dot(hot, mixed[0:windows].reshape(windows * PAD, D)).astype(BF)
        branch = dot(taken, weights[...].reshape(D, D))
        return (base + norm_rows(branch, gain)).astype(BF)

    g_fine_qkv.finish()
    g_fine_out.spread()
    g_merge.spread()
    arrived(row_copies)
    frame = framed(0, (0, 3), 0, 0, pool, ABOVE, 544)
    project((0, 3), frame, fine_qkv, fine_scale)
    attend(0, (0, 3), lambda w: w, 12)

    arrived(side_copies)
    near = pool[OWN : OWN + 576, :]
    to_below_c[...] = dot(picked(9, 112, 0, OWN, 576), near).astype(BF)
    to_above_c[...] = dot(picked(10, 112, 0, OWN, 576), near).astype(BF)
    row_copies = [
        send(to_below_c, pool.at[pl.ds(ABOVE_C, 112)], along_lat(1)),
        send(to_above_c, pool.at[pl.ds(BELOW_C, 112)], along_lat(-1)),
    ]
    g_coarse_qkv.start()
    g_coarse_out.start()
    frame = framed(0, (3, 2), 0, 0, pool, OWN, 576)
    project((3, 2), frame, fine_qkv, fine_scale)
    attend(0, (3, 2), lambda w: 1, 12)

    frame = framed(0, (5, 4), 0, 0, pool, 0, ABOVE_C)
    arrived(row_copies)
    frame = frame + framed(0, (5, 4), 0, 0, pool, ABOVE_C, POOL - ABOVE_C)
    g_fine_out.share()
    g_merge.share()
    project((5, 4), frame, fine_qkv, fine_scale)
    attend(0, (5, 4), lambda w: 2 * (w // 2), 12)
    g_fine_out.finish()
    in_quads = dot(picked(1, 320, 0, OWN, 288), tokens[...])
    fine_after[...] = finish(0, 9, 1, 320, 1, fine_out, in_quads, fine_gain[...])
    g_coarse_qkv.pair()
    g_coarse_out.pair()
    g_merge.finish()
    merged = jnp.zeros((PAD, D), F32)
    for p in range(4):
        rows = merge[2 * p : 2 * p + 2].reshape(D, D)
        merged = merged + dot(fine_after[PAD * p : PAD * p + PAD, :], rows)
    coarse_pool[0:PAD, :] = norm_rows(merged, merge_gain[...]).astype(BF)
    mine = coarse_pool.at[pl.ds(0, PAD)]
    side_copies = [
        send(mine, coarse_pool.at[pl.ds(C_LEFT, PAD)], along_lon(1)),
        send(mine, coarse_pool.at[pl.ds(C_RIGHT, PAD)], along_lon(-1)),
    ]
    row_copies = [
        send(mine, coarse_pool.at[pl.ds(C_ABOVE, PAD)], along_lat(1)),
        send(mine, coarse_pool.at[pl.ds(C_BELOW, PAD)], along_lat(-1)),
    ]
    g_coarse_qkv.spread()
    g_coarse_out.spread()
    arrived(side_copies)
    near = coarse_pool[0 : 3 * PAD, :]
    to_below_k[...] = dot(picked(11, 112, 3, 0, 3 * PAD), near).astype(BF)
    to_above_k[...] = dot(picked(12, 112, 3, 0, 3 * PAD), near).astype(BF)
    row_copies += [
        send(to_below_k, coarse_pool.at[pl.ds(C_ABOVE_C, 112)], along_lat(1)),
        send(to_above_k, coarse_pool.at[pl.ds(C_BELOW_C, 112)], along_lat(-1)),
    ]
    g_coarse_qkv.share()
    g_coarse_out.share()
    frame = framed(1, (0, 4), 2, 3, coarse_pool, 0, C_ABOVE)
    g_coarse_qkv.finish()
    arrived(row_copies[:2])
    frame = frame + framed(1, (0, 4), 2, 3, coarse_pool, C_ABOVE, C_ABOVE_C - C_ABOVE)
    arrived(row_copies[2:])
    corners = CPOOL - C_ABOVE_C
    frame = frame + framed(1, (0, 4), 2, 3, coarse_pool, C_ABOVE_C, corners)
    project((0, 4), frame, coarse_qkv, coarse_scale)
    attend(1, (0, 4), lambda w: w // 2, 6)
    g_coarse_out.finish()
    base = coarse_pool[0:PAD, :].astype(F32)
    coarse_after = finish(1, 4, 3, PAD, 4, coarse_out, base, coarse_gain[...]).astype(F32)
    for p in range(4):
        part = fine_after[PAD * p : PAD * p + PAD, :].astype(F32) + coarse_after
        fine_after[PAD * p : PAD * p + PAD, :] = part.astype(BF)
    out[...] = dot(picked(4, 288, 2, 0, 320), fine_after[...]).astype(BF)
    for copy in sent:
        copy.wait_send()


COPIES = 12 + 21 + 12 + 23 + 12 + 12


def per_device(
    tokens,
    fine_qkv,
    fine_out,
    fine_scale,
    fine_table,
    fine_gain,
    merge_weight,
    merge_gain,
    coarse_qkv,
    coarse_out,
    coarse_scale,
    coarse_table,
    coarse_gain,
    shifts,
    bias_index,
):
    by_row, by_column = code_tables()
    rows, columns, width = tokens.shape
    smem = pl.BlockSpec(memory_space=pltpu.SMEM)
    vmem = pl.BlockSpec(memory_space=pltpu.VMEM)
    hbm = pl.BlockSpec(memory_space=pltpu.HBM)
    result = pl.pallas_call(
        kernel,
        out_shape=jax.ShapeDtypeStruct((rows * columns, width), BF),
        in_specs=[smem] * 3 + [hbm] * 14,
        out_specs=vmem,
        scratch_shapes=[
            pltpu.VMEM((8, 2, 32, 1536), BF),
            pltpu.VMEM((8, 2, 32, 512), BF),
            pltpu.VMEM((8, 2, 128, 512), BF),
            pltpu.VMEM((8, 2, 32, 1536), BF),
            pltpu.VMEM((8, 2, 32, 512), BF),
            pltpu.VMEM((POOL, D), BF),
            pltpu.VMEM((144, D), BF),
            pltpu.VMEM((144, D), BF),
            pltpu.VMEM((128, D), BF),
            pltpu.VMEM((128, D), BF),
            pltpu.VMEM((112, D), BF),
            pltpu.VMEM((112, D), BF),
            pltpu.VMEM((9, PAD, D), BF),
            pltpu.VMEM((9, PAD, D), BF),
            pltpu.VMEM((9, PAD, D), BF),
            pltpu.VMEM((9, PAD, D), BF),
            pltpu.VMEM((320, D), BF),
            pltpu.VMEM((CPOOL, D), BF),
            pltpu.VMEM((16, PAD, 128), F32),
            pltpu.VMEM((288, D), BF),
            pltpu.VMEM((HEADS, 253), F32),
            pltpu.VMEM((HEADS, 253), F32),
            pltpu.VMEM((WIN, WIN), jnp.int32),
            pltpu.VMEM((1, D), F32),
            pltpu.VMEM((1, D), F32),
            pltpu.VMEM((1, D), F32),
            pltpu.VMEM((8, 1152), jnp.int32),
            pltpu.VMEM((720, 128), jnp.int32),
            pltpu.VMEM((16, 256), F32),
            pltpu.VMEM((112, D), BF),
            pltpu.VMEM((112, D), BF),
            pltpu.SemaphoreType.DMA((COPIES,)),
            pltpu.SemaphoreType.DMA((COPIES,)),
            pltpu.SemaphoreType.DMA((20,)),
        ],
        compiler_params=pltpu.CompilerParams(
            collective_id=0, has_side_effects=True, vmem_limit_bytes=64 << 20
        ),
    )(
        shifts,
        fine_scale,
        coarse_scale,
        tokens.reshape(rows * columns, width),
        fine_qkv,
        fine_out,
        merge_weight,
        coarse_qkv,
        coarse_out,
        fine_table.T,
        coarse_table.T,
        bias_index,
        fine_gain.reshape(1, -1),
        merge_gain.reshape(1, -1),
        coarse_gain.reshape(1, -1),
        jnp.asarray(by_row),
        jnp.asarray(by_column),
    )
    return result.reshape(rows, columns, width)


def solution(mesh):
    placed = (
        P("lat", "lon", None),
        P("lat", None),
        P("lat", None),
        P(),
        P(),
        P(),
        P("lat", None),
        P(),
        P("lat", None),
        P("lat", None),
        P(),
        P(),
        P(),
        P(),
        P(),
    )
    return jax.shard_map(
        per_device, mesh=mesh, in_specs=placed, out_specs=P("lat", "lon", None), check_vma=False
    )
```

```python
import functools

import jax
import jax.numpy as jnp
import numpy as np
from jax import lax
from jax.experimental import pallas as pl
from jax.experimental.pallas import tpu as pltpu
from jax.sharding import PartitionSpec as P

MESH = pl.DeviceIdType.MESH
HEADS = 8
WLAT = 6
WLON = 12
WIN = 72
PAD = 80
D = 512
BF = jnp.bfloat16
F32 = jnp.float32

ABOVE, BELOW, OWN, LEFT, RIGHT, ABOVE_C, BELOW_C = 0, 128, 256, 544, 688, 832, 944
POOL = 1056
C_LEFT, C_RIGHT, C_ABOVE, C_BELOW, C_ABOVE_C, C_BELOW_C = 80, 160, 240, 320, 400, 512
CPOOL = 624
FINE_WINDOWS = [(0, 1), (1, 1), (2, 1), (1, 0), (1, 2), (0, 0), (0, 2), (2, 0), (2, 2)]
COARSE_WINDOWS = [(0, 0), (0, 1), (1, 0), (1, 1)]
LOG2E = 1.4426950408889634
NOWHERE = -200000
UNUSED = -100000


def code(row, column):
    return (row + 32) * 128 + column + 32


def padded_codes(places, length, fill):
    out = np.full((length,), fill, np.int32)
    out[: len(places)] = [code(r, c) for r, c in places]
    return out


def grid_places(rows, columns):
    return [(r, c) for r in rows for c in columns]


def frame_places(windows):
    parts = []
    for a, b in windows:
        rows = range(WLAT * a - WLAT, WLAT * a)
        columns = range(WLON * b - WLON, WLON * b)
        parts.append(grid_places(rows, columns))
    return parts


def blocks_of(parts, block, fill):
    return np.concatenate([padded_codes(p, block, fill) for p in parts])


def code_tables():
    own = grid_places(range(12), range(24))
    far_left = grid_places(range(12), range(-11, 0))
    far_right = grid_places(range(12), range(24, 35))
    sides = list(range(-11, 0)) + list(range(24, 35))
    above, below = range(-5, 0), range(12, 17)
    pool = np.concatenate(
        [
            padded_codes(grid_places(above, range(24)), 128, NOWHERE),
            padded_codes(grid_places(below, range(24)), 128, NOWHERE),
            padded_codes(own, 288, NOWHERE),
            padded_codes(far_left, 144, NOWHERE),
            padded_codes(far_right, 144, NOWHERE),
            padded_codes(grid_places(above, sides), 112, NOWHERE),
            padded_codes(grid_places(below, sides), 112, NOWHERE),
        ]
    )
    quads = [
        [(2 * a + i, 2 * b + j) for a in range(6) for b in range(12)]
        for j in range(2)
        for i in range(2)
    ]
    coarse_sides = list(range(-11, 0)) + list(range(12, 23))
    coarse_tiles = [(0, 0), (0, -1), (0, 1), (-1, 0), (1, 0)]
    coarse_pool = np.concatenate(
        [
            padded_codes(
                grid_places(range(6 * i, 6 * i + 6), range(12 * j, 12 * j + 12)), PAD, NOWHERE
            )
            for i, j in coarse_tiles
        ]
        + [
            padded_codes(grid_places(range(-5, 0), coarse_sides), 112, NOWHERE),
            padded_codes(grid_places(range(6, 11), coarse_sides), 112, NOWHERE),
        ]
    )
    fine_frame, coarse_frame = frame_places(FINE_WINDOWS), frame_places(COARSE_WINDOWS)
    by_row = np.full((8, 1152), NOWHERE, np.int32)
    for at, values in enumerate(
        [
            pool,
            blocks_of(fine_frame, PAD, NOWHERE),
            blocks_of(quads, PAD, NOWHERE),
            coarse_pool,
            blocks_of(coarse_frame, PAD, NOWHERE),
        ]
    ):
        by_row[at, : len(values)] = values
    by_column = np.full((720, 128), UNUSED, np.int32)
    for at, values in enumerate(
        [
            blocks_of(fine_frame, PAD, UNUSED),
            blocks_of(quads, PAD, UNUSED),
            blocks_of(coarse_frame, PAD, UNUSED),
            blocks_of([grid_places(range(6), range(12))], PAD, UNUSED),
            padded_codes(own, 288, UNUSED),
            padded_codes(grid_places(range(12), range(13, 24)), 144, UNUSED),
            padded_codes(grid_places(range(12), range(11)), 144, UNUSED),
            padded_codes(grid_places(range(7, 12), range(24)), 128, UNUSED),
            padded_codes(grid_places(range(5), range(24)), 128, UNUSED),
            padded_codes(grid_places(range(7, 12), sides), 112, UNUSED),
            padded_codes(grid_places(range(5), sides), 112, UNUSED),
            padded_codes(grid_places(range(1, 6), coarse_sides), 112, UNUSED),
            padded_codes(grid_places(range(5), coarse_sides), 112, UNUSED),
        ]
    ):
        by_column[: len(values), at] = values
    return by_row, by_column


def norm_rows(values, gain):
    middle = jnp.mean(values, axis=-1, keepdims=True)
    centered = values - middle
    spread = jnp.mean(centered * centered, axis=-1, keepdims=True)
    return centered * lax.rsqrt(spread + 1e-05) * gain


def dot(a, b):
    return jnp.dot(a, b, preferred_element_type=F32)


def dot_nt(a, b):
    return lax.dot_general(a, b, (((1,), (1,)), ((), ())), preferred_element_type=F32)


def kernel(
    shifts,
    fine_scale,
    coarse_scale,
    hbm_tokens,
    w_fine_qkv,
    w_fine_out,
    w_merge,
    w_coarse_qkv,
    w_coarse_out,
    hbm_fine_table,
    hbm_coarse_table,
    hbm_bias_index,
    hbm_fine_gain,
    hbm_merge_gain,
    hbm_coarse_gain,
    hbm_by_row,
    hbm_by_column,
    out,
    fine_qkv,
    fine_out,
    merge,
    coarse_qkv,
    coarse_out,
    pool,
    to_right,
    to_left,
    to_below,
    to_above,
    to_below_c,
    to_above_c,
    query,
    key,
    value,
    mixed,
    fine_after,
    coarse_pool,
    bias,
    tokens,
    fine_table,
    coarse_table,
    bias_index,
    fine_gain,
    merge_gain,
    coarse_gain,
    by_row,
    by_column,
    tables,
    to_below_k,
    to_above_k,
    send_sem,
    recv_sem,
    local_sem,
):
    lat, lon = lax.axis_index("lat"), lax.axis_index("lon")
    core, z_lo = lat % 2, lat // 2
    x, z_hi, y = lon // 8, (lon // 4) % 2, lon % 4
    z = z_hi * 8 + z_lo

    def place(x, y, z, core):
        x, y, z = (x + 4) % 4, (y + 4) % 4, (z + 16) % 16
        return ((z % 8) * 2 + core, x * 8 + (z // 8) * 4 + y)

    def along_z(d):
        return place(x, y, z + d, core)

    def along_x(d):
        return place(x + d, y, z, core)

    def along_y(d):
        return place(x, y + d, z, core)

    line = z * 2 + core

    def along_lat(d):
        spot = (line + d + 32) % 32
        return place(x, y, spot // 2, spot % 2)

    def along_lon(d):
        return (lat, (lon + d + 32) % 32)

    sibling = place(x, y, z, 1 - core)
    opposite = 4 - 8 * core
    hops = (opposite, 3, -3, 2, -2, 1, -1)

    barrier = pltpu.get_barrier_semaphore()
    senders = [along_z(-d) for d in hops]
    senders += [along_x(d) for d in (1, -1, 2)] + [along_y(d) for d in (1, -1, 2)]
    senders += [sibling, along_lon(1), along_lon(-1), along_lat(1), along_lat(-1)]
    for device in senders:
        pl.semaphore_signal(barrier, inc=1, device_id=device, device_id_type=MESH)

    local_count = [0]

    def bring(source, target):
        at = local_count[0]
        local_count[0] += 1
        copy = pltpu.make_async_copy(source, target, local_sem.at[at])
        copy.start()
        return copy

    first = [
        bring(hbm_tokens, tokens),
        bring(hbm_by_row, by_row),
        bring(hbm_by_column, by_column),
    ]
    later = [
        bring(hbm_fine_table, fine_table),
        bring(hbm_coarse_table, coarse_table),
        bring(hbm_bias_index, bias_index),
        bring(hbm_fine_gain, fine_gain),
        bring(hbm_merge_gain, merge_gain),
        bring(hbm_coarse_gain, coarse_gain),
    ]

    def picked(column, rows, row_at, first, width, offset=0):
        left = by_column[0:rows, column : column + 1] + offset
        right = by_row[row_at : row_at + 1, first : first + width]
        return jnp.where(left == right, 1.0, 0.0).astype(BF)

    counter = [0]
    sent = []

    def send(source, target, device):
        at = counter[0]
        counter[0] += 1
        copy = pltpu.make_async_remote_copy(
            src_ref=source,
            dst_ref=target,
            send_sem=send_sem.at[at],
            recv_sem=recv_sem.at[at],
            device_id=device,
            device_id_type=MESH,
        )
        copy.start()
        sent.append(copy)
        return copy

    def arrived(copies):
        for copy in copies:
            copy.wait_recv()

    class Gather:
        def __init__(self, shard, whole, halves):
            self.shard, self.whole, self.halves = shard, whole, halves

        def start(self):
            self.ready, self.waits = [], []
            for axis, part, pair_axis, small in self.halves:
                rows, columns = small
                source = self.shard.at[rows, columns]
                target = self.whole.at[z_lo, core, rows, columns]
                self.ready.append(bring(source, target))
                for d in hops:
                    self.waits.append(send(source, target, along_z(d)))

        def begun(self):
            for copy in self.ready:
                copy.wait()
            arrived(self.waits)
            self.ready, self.waits = [], []

        def pair(self):
            self.begun()
            for axis, part, pair_axis, (rows, columns) in self.halves:
                area = self.whole.at[:, core, rows, columns]
                self.waits.append(send(area, area, pair_axis(1)))

        def spread(self):
            self.begun()
            for axis, (rows, columns), pair_axis, small in self.halves:
                area = self.whole.at[:, core, rows, columns]
                for d in (1, -1, 2):
                    self.waits.append(send(area, area, axis(d)))

        def share(self):
            arrived(self.waits)
            part = self.whole.at[:, core]
            self.waits = [send(part, part, sibling)]

        def finish(self):
            arrived(self.waits)

    def by_x(part):
        return along_x, part(x), along_y, part(x, y % 2)

    def by_y(part):
        return along_y, part(y), along_x, part(y, x % 2)

    def corner(first, width):
        def part(g, half=None):
            rows = pl.ds(pl.multiple_of((g // 2) * 16, 16), 16)
            at, wide = first + (g % 2) * width, width
            if half is not None:
                at, wide = at + half * (width // 2), width // 2
            return rows, pl.ds(pl.multiple_of(at, 128), wide)

        return part

    def band(first, width):
        def part(g, half=None):
            if half is None:
                return pl.ds(pl.multiple_of(g * 32, 32), 32), pl.ds(first, width)
            return pl.ds(pl.multiple_of(g * 32 + half * 16, 16), 16), pl.ds(first, width)

        return part

    def quarters(axis, g, first):
        part = corner(first, 384)(g)
        return axis, part, None, part

    g_fine_qkv = Gather(
        w_fine_qkv, fine_qkv, [quarters(along_x, x, 0), quarters(along_y, y, 768)]
    )
    g_fine_out = Gather(w_fine_out, fine_out, [by_x(corner(0, 256))])
    g_merge = Gather(w_merge, merge, [by_x(band(0, 256)), by_y(band(256, 256))])
    g_coarse_qkv = Gather(w_coarse_qkv, coarse_qkv, [by_x(corner(0, 768))])
    g_coarse_out = Gather(w_coarse_out, coarse_out, [by_y(corner(0, 256))])

    pl.semaphore_wait(barrier, len(senders))
    g_fine_qkv.start()
    g_fine_out.start()
    g_merge.start()
    for copy in first:
        copy.wait()
    own = tokens[...]
    to_right[...] = dot(picked(5, 144, 0, OWN, 288), own).astype(BF)
    to_left[...] = dot(picked(6, 144, 0, OWN, 288), own).astype(BF)
    to_below[...] = dot(picked(7, 128, 0, OWN, 288), own).astype(BF)
    to_above[...] = dot(picked(8, 128, 0, OWN, 288), own).astype(BF)
    pool[OWN : OWN + 288, :] = own

    g_fine_qkv.spread()
    side_copies = [
        send(to_right, pool.at[pl.ds(LEFT, 144)], along_lon(1)),
        send(to_left, pool.at[pl.ds(RIGHT, 144)], along_lon(-1)),
    ]
    row_copies = [
        send(to_below, pool.at[pl.ds(ABOVE, 128)], along_lat(1)),
        send(to_above, pool.at[pl.ds(BELOW, 128)], along_lat(-1)),
    ]
    bias[...] = jnp.zeros((16, PAD, 128), F32)
    tables[...] = jnp.zeros((16, 256), F32)
    for copy in later:
        copy.wait()
    tables[0:HEADS, 0:253] = fine_table[...]
    tables[HEADS : 2 * HEADS, 0:253] = coarse_table[...]
    table = tables[...]
    top = table.astype(BF)
    rest = table - top.astype(F32)
    middle = rest.astype(BF)
    bottom = (rest - middle.astype(F32)).astype(BF)
    table_parts = jnp.concatenate([top, middle, bottom], axis=0)
    levels = lax.broadcasted_iota(jnp.int32, (256, WIN), 0)

    def bias_rows(group, carry):
        rows = bias_index[pl.ds(pl.multiple_of(group * 8, 8), 8), :]
        for i in range(8):
            hot = jnp.where(levels == rows[i : i + 1, :], 1.0, 0.0).astype(BF)
            parts = dot(table_parts, hot)
            looked = (parts[0:16] + parts[16:32] + parts[32:48]) * LOG2E
            bias[:, pl.ds(group * 8 + i, 1), 0:WIN] = looked.reshape(16, 1, WIN)
        return carry

    lax.fori_loop(0, WIN // 8, bias_rows, 0)

    g_fine_qkv.share()
    g_fine_out.pair()
    g_merge.pair()

    lane = lax.broadcasted_iota(jnp.int32, (1, 128), 1)
    low = jnp.where(lane < 64, 1.0, 0.0).astype(BF)
    high = jnp.where(lane < 64, 0.0, 1.0).astype(BF)
    position = lax.broadcasted_iota(jnp.int32, (PAD, 128), 0)
    row_of = jnp.zeros((PAD, 128), jnp.int32)
    for r in range(1, WLAT):
        row_of = row_of + jnp.where(position >= WLON * r, 1, 0)
    ones_row = lax.broadcasted_iota(jnp.int32, (256, 256), 0) // 64
    ones_column = lax.broadcasted_iota(jnp.int32, (256, 256), 1) // 64
    same_head = jnp.where(ones_row == ones_column, 1.0, 0.0).astype(BF)

    def scale_row(scale):
        head_of = lax.broadcasted_iota(jnp.int32, (1, D), 1) // 64
        row = jnp.zeros((1, D), F32)
        for n in range(HEADS):
            row = jnp.where(head_of == n, scale[n] * LOG2E, row)
        return row

    def framed(level, windows, column, row_at, cells, first, width):
        offset = shifts[level, 0] * 128 + shifts[level, 1]
        at, count = windows
        left = by_column[at * PAD : (at + count) * PAD, column : column + 1] + offset
        right = by_row[row_at : row_at + 1, first : first + width]
        hot = jnp.where(left == right, 1.0, 0.0).astype(BF)
        return dot(hot, cells[first : first + width, :])

    def project(windows, cells, weights, scale):
        scales = scale_row(scale)
        at, count = windows
        frame = cells.astype(BF)
        for n in range(6):
            block = weights[:, :, :, 256 * n : 256 * n + 256].reshape(D, 256)
            rounded = dot(frame, block).astype(BF)
            columns = slice(256 * (n % 2), 256 * (n % 2) + 256)
            if n < 4:
                full = rounded.astype(F32)
                square = dot((full * full).astype(BF), same_head)
                full = full * lax.rsqrt(square + 1e-06)
                if n < 2:
                    full = full * scales[:, columns]
                rounded = full.astype(BF)
            target = (query, key, value)[n // 2]
            target[at : at + count, :, columns] = rounded.reshape(count, PAD, 256)

    def attend(level, windows, row_block, rows_here):
        first_row = lat * rows_here + shifts[level, 0] - WLAT
        at, count = windows

        def one(w, carry):
            latitude = row_of + (first_row + WLAT * row_block(w))
            here = (latitude >= 0) & (latitude < rows_here * 16) & (position < WIN)
            keep = jnp.where(here, 1.0, 0.0).astype(BF)
            for p in range(HEADS // 2):
                columns = slice(128 * p, 128 * p + 128)
                q = query[at + w, :, columns]
                pair = jnp.concatenate([q * low, q * high], axis=0)
                scores = dot_nt(pair, key[at + w, :, columns])
                own_bias = bias[8 * level + 2 * p : 8 * level + 2 * p + 2, :, 0:PAD]
                powers = jnp.exp2(scores + own_bias.reshape(2 * PAD, PAD)).astype(BF)
                kept = jnp.concatenate([value[at + w, :, columns] * keep, keep], axis=1)
                both = dot(powers, kept)
                mine = jnp.where(lane < 64, both[0:PAD, 0:128], both[PAD : 2 * PAD, 0:128])
                total = jnp.where(lane < 64, both[0:PAD, 128:256], both[PAD : 2 * PAD, 128:256])
                taken = mine / total
                mixed[at + w, :, columns] = taken.astype(BF)
            return carry

        lax.fori_loop(0, count, one, 0, unroll=True)

    def finish(level, windows, column, rows, row_at, weights, base, gain):
        offset = shifts[level, 0] * 128 + shifts[level, 1]
        left = by_column[0:rows, column : column + 1] - offset
        right = by_row[row_at : row_at + 1, 0 : windows * PAD]
        hot = jnp.where(left == right, 1.0, 0.0).astype(BF)
        taken = dot(hot, mixed[0:windows].reshape(windows * PAD, D)).astype(BF)
        branch = dot(taken, weights[...].reshape(D, D))
        return (base + norm_rows(branch, gain)).astype(BF)

    g_fine_qkv.finish()
    g_fine_out.spread()
    g_merge.spread()
    arrived(row_copies)
    frame = framed(0, (0, 3), 0, 0, pool, ABOVE, 544)
    project((0, 3), frame, fine_qkv, fine_scale)
    attend(0, (0, 3), lambda w: w, 12)

    arrived(side_copies)
    near = pool[OWN : OWN + 576, :]
    to_below_c[...] = dot(picked(9, 112, 0, OWN, 576), near).astype(BF)
    to_above_c[...] = dot(picked(10, 112, 0, OWN, 576), near).astype(BF)
    row_copies = [
        send(to_below_c, pool.at[pl.ds(ABOVE_C, 112)], along_lat(1)),
        send(to_above_c, pool.at[pl.ds(BELOW_C, 112)], along_lat(-1)),
    ]
    frame = framed(0, (3, 2), 0, 0, pool, OWN, 576)
    project((3, 2), frame, fine_qkv, fine_scale)
    attend(0, (3, 2), lambda w: 1, 12)
    g_coarse_qkv.start()
    g_coarse_out.start()

    frame = framed(0, (5, 4), 0, 0, pool, 0, ABOVE_C)
    arrived(row_copies)
    frame = frame + framed(0, (5, 4), 0, 0, pool, ABOVE_C, POOL - ABOVE_C)
    g_fine_out.share()
    g_merge.share()
    project((5, 4), frame, fine_qkv, fine_scale)
    attend(0, (5, 4), lambda w: 2 * (w // 2), 12)
    g_fine_out.finish()
    in_quads = dot(picked(1, 320, 0, OWN, 288), tokens[...])
    fine_after[...] = finish(0, 9, 1, 320, 1, fine_out, in_quads, fine_gain[...])
    g_coarse_qkv.pair()
    g_coarse_out.pair()
    g_merge.finish()
    merged = jnp.zeros((PAD, D), F32)
    for p in range(4):
        rows = merge[2 * p : 2 * p + 2].reshape(D, D)
        merged = merged + dot(fine_after[PAD * p : PAD * p + PAD, :], rows)
    coarse_pool[0:PAD, :] = norm_rows(merged, merge_gain[...]).astype(BF)
    mine = coarse_pool.at[pl.ds(0, PAD)]
    side_copies = [
        send(mine, coarse_pool.at[pl.ds(C_LEFT, PAD)], along_lon(1)),
        send(mine, coarse_pool.at[pl.ds(C_RIGHT, PAD)], along_lon(-1)),
    ]
    row_copies = [
        send(mine, coarse_pool.at[pl.ds(C_ABOVE, PAD)], along_lat(1)),
        send(mine, coarse_pool.at[pl.ds(C_BELOW, PAD)], along_lat(-1)),
    ]
    g_coarse_qkv.spread()
    g_coarse_out.spread()
    arrived(side_copies)
    near = coarse_pool[0 : 3 * PAD, :]
    to_below_k[...] = dot(picked(11, 112, 3, 0, 3 * PAD), near).astype(BF)
    to_above_k[...] = dot(picked(12, 112, 3, 0, 3 * PAD), near).astype(BF)
    row_copies += [
        send(to_below_k, coarse_pool.at[pl.ds(C_ABOVE_C, 112)], along_lat(1)),
        send(to_above_k, coarse_pool.at[pl.ds(C_BELOW_C, 112)], along_lat(-1)),
    ]
    g_coarse_qkv.share()
    g_coarse_out.share()
    frame = framed(1, (0, 4), 2, 3, coarse_pool, 0, C_ABOVE)
    g_coarse_qkv.finish()
    arrived(row_copies[:2])
    frame = frame + framed(1, (0, 4), 2, 3, coarse_pool, C_ABOVE, C_ABOVE_C - C_ABOVE)
    arrived(row_copies[2:])
    corners = CPOOL - C_ABOVE_C
    frame = frame + framed(1, (0, 4), 2, 3, coarse_pool, C_ABOVE_C, corners)
    project((0, 4), frame, coarse_qkv, coarse_scale)
    attend(1, (0, 4), lambda w: w // 2, 6)
    g_coarse_out.finish()
    base = coarse_pool[0:PAD, :].astype(F32)
    coarse_after = finish(1, 4, 3, PAD, 4, coarse_out, base, coarse_gain[...]).astype(F32)
    for p in range(4):
        part = fine_after[PAD * p : PAD * p + PAD, :].astype(F32) + coarse_after
        fine_after[PAD * p : PAD * p + PAD, :] = part.astype(BF)
    out[...] = dot(picked(4, 288, 2, 0, 320), fine_after[...]).astype(BF)
    for copy in sent:
        copy.wait_send()


COPIES = 12 + 21 + 12 + 23 + 12 + 12


def per_device(
    tokens,
    fine_qkv,
    fine_out,
    fine_scale,
    fine_table,
    fine_gain,
    merge_weight,
    merge_gain,
    coarse_qkv,
    coarse_out,
    coarse_scale,
    coarse_table,
    coarse_gain,
    shifts,
    bias_index,
):
    by_row, by_column = code_tables()
    rows, columns, width = tokens.shape
    smem = pl.BlockSpec(memory_space=pltpu.SMEM)
    vmem = pl.BlockSpec(memory_space=pltpu.VMEM)
    hbm = pl.BlockSpec(memory_space=pltpu.HBM)
    result = pl.pallas_call(
        kernel,
        out_shape=jax.ShapeDtypeStruct((rows * columns, width), BF),
        in_specs=[smem] * 3 + [hbm] * 14,
        out_specs=vmem,
        scratch_shapes=[
            pltpu.VMEM((8, 2, 32, 1536), BF),
            pltpu.VMEM((8, 2, 32, 512), BF),
            pltpu.VMEM((8, 2, 128, 512), BF),
            pltpu.VMEM((8, 2, 32, 1536), BF),
            pltpu.VMEM((8, 2, 32, 512), BF),
            pltpu.VMEM((POOL, D), BF),
            pltpu.VMEM((144, D), BF),
            pltpu.VMEM((144, D), BF),
            pltpu.VMEM((128, D), BF),
            pltpu.VMEM((128, D), BF),
            pltpu.VMEM((112, D), BF),
            pltpu.VMEM((112, D), BF),
            pltpu.VMEM((9, PAD, D), BF),
            pltpu.VMEM((9, PAD, D), BF),
            pltpu.VMEM((9, PAD, D), BF),
            pltpu.VMEM((9, PAD, D), BF),
            pltpu.VMEM((320, D), BF),
            pltpu.VMEM((CPOOL, D), BF),
            pltpu.VMEM((16, PAD, 128), F32),
            pltpu.VMEM((288, D), BF),
            pltpu.VMEM((HEADS, 253), F32),
            pltpu.VMEM((HEADS, 253), F32),
            pltpu.VMEM((WIN, WIN), jnp.int32),
            pltpu.VMEM((1, D), F32),
            pltpu.VMEM((1, D), F32),
            pltpu.VMEM((1, D), F32),
            pltpu.VMEM((8, 1152), jnp.int32),
            pltpu.VMEM((720, 128), jnp.int32),
            pltpu.VMEM((16, 256), F32),
            pltpu.VMEM((112, D), BF),
            pltpu.VMEM((112, D), BF),
            pltpu.SemaphoreType.DMA((COPIES,)),
            pltpu.SemaphoreType.DMA((COPIES,)),
            pltpu.SemaphoreType.DMA((20,)),
        ],
        compiler_params=pltpu.CompilerParams(
            collective_id=0, has_side_effects=True, vmem_limit_bytes=64 << 20
        ),
    )(
        shifts,
        fine_scale,
        coarse_scale,
        tokens.reshape(rows * columns, width),
        fine_qkv,
        fine_out,
        merge_weight,
        coarse_qkv,
        coarse_out,
        fine_table.T,
        coarse_table.T,
        bias_index,
        fine_gain.reshape(1, -1),
        merge_gain.reshape(1, -1),
        coarse_gain.reshape(1, -1),
        jnp.asarray(by_row),
        jnp.asarray(by_column),
    )
    return result.reshape(rows, columns, width)


def solution(mesh):
    placed = (
        P("lat", "lon", None),
        P("lat", None),
        P("lat", None),
        P(),
        P(),
        P(),
        P("lat", None),
        P(),
        P("lat", None),
        P("lat", None),
        P(),
        P(),
        P(),
        P(),
        P(),
    )
    return jax.shard_map(
        per_device, mesh=mesh, in_specs=placed, out_specs=P("lat", "lon", None), check_vma=False
    )
```

```python
import functools

import jax
import jax.numpy as jnp
import numpy as np
from jax import lax
from jax.experimental import pallas as pl
from jax.experimental.pallas import tpu as pltpu
from jax.sharding import PartitionSpec as P

MESH = pl.DeviceIdType.MESH
HEADS = 8
WLAT = 6
WLON = 12
WIN = 72
PAD = 80
D = 512
BF = jnp.bfloat16
F32 = jnp.float32

ABOVE, BELOW, OWN, LEFT, RIGHT, ABOVE_C, BELOW_C = 0, 128, 256, 544, 688, 832, 944
POOL = 1056
C_LEFT, C_RIGHT, C_ABOVE, C_BELOW, C_ABOVE_C, C_BELOW_C = 80, 160, 240, 320, 400, 512
CPOOL = 624
FINE_WINDOWS = [(0, 1), (1, 1), (2, 1), (1, 0), (1, 2), (0, 0), (0, 2), (2, 0), (2, 2)]
COARSE_WINDOWS = [(0, 0), (0, 1), (1, 0), (1, 1)]
LOG2E = 1.4426950408889634
NOWHERE = -200000
UNUSED = -100000


def code(row, column):
    return (row + 32) * 128 + column + 32


def padded_codes(places, length, fill):
    out = np.full((length,), fill, np.int32)
    out[: len(places)] = [code(r, c) for r, c in places]
    return out


def grid_places(rows, columns):
    return [(r, c) for r in rows for c in columns]


def frame_places(windows):
    parts = []
    for a, b in windows:
        rows = range(WLAT * a - WLAT, WLAT * a)
        columns = range(WLON * b - WLON, WLON * b)
        parts.append(grid_places(rows, columns))
    return parts


def blocks_of(parts, block, fill):
    return np.concatenate([padded_codes(p, block, fill) for p in parts])


def code_tables():
    own = grid_places(range(12), range(24))
    far_left = grid_places(range(12), range(-11, 0))
    far_right = grid_places(range(12), range(24, 35))
    sides = list(range(-11, 0)) + list(range(24, 35))
    above, below = range(-5, 0), range(12, 17)
    pool = np.concatenate(
        [
            padded_codes(grid_places(above, range(24)), 128, NOWHERE),
            padded_codes(grid_places(below, range(24)), 128, NOWHERE),
            padded_codes(own, 288, NOWHERE),
            padded_codes(far_left, 144, NOWHERE),
            padded_codes(far_right, 144, NOWHERE),
            padded_codes(grid_places(above, sides), 112, NOWHERE),
            padded_codes(grid_places(below, sides), 112, NOWHERE),
        ]
    )
    quads = [
        [(2 * a + i, 2 * b + j) for a in range(6) for b in range(12)]
        for j in range(2)
        for i in range(2)
    ]
    coarse_sides = list(range(-11, 0)) + list(range(12, 23))
    coarse_tiles = [(0, 0), (0, -1), (0, 1), (-1, 0), (1, 0)]
    coarse_pool = np.concatenate(
        [
            padded_codes(
                grid_places(range(6 * i, 6 * i + 6), range(12 * j, 12 * j + 12)), PAD, NOWHERE
            )
            for i, j in coarse_tiles
        ]
        + [
            padded_codes(grid_places(range(-5, 0), coarse_sides), 112, NOWHERE),
            padded_codes(grid_places(range(6, 11), coarse_sides), 112, NOWHERE),
        ]
    )
    fine_frame, coarse_frame = frame_places(FINE_WINDOWS), frame_places(COARSE_WINDOWS)
    by_row = np.full((8, 1152), NOWHERE, np.int32)
    for at, values in enumerate(
        [
            pool,
            blocks_of(fine_frame, PAD, NOWHERE),
            blocks_of(quads, PAD, NOWHERE),
            coarse_pool,
            blocks_of(coarse_frame, PAD, NOWHERE),
        ]
    ):
        by_row[at, : len(values)] = values
    by_column = np.full((720, 128), UNUSED, np.int32)
    for at, values in enumerate(
        [
            blocks_of(fine_frame, PAD, UNUSED),
            blocks_of(quads, PAD, UNUSED),
            blocks_of(coarse_frame, PAD, UNUSED),
            blocks_of([grid_places(range(6), range(12))], PAD, UNUSED),
            padded_codes(own, 288, UNUSED),
            padded_codes(grid_places(range(12), range(13, 24)), 144, UNUSED),
            padded_codes(grid_places(range(12), range(11)), 144, UNUSED),
            padded_codes(grid_places(range(7, 12), range(24)), 128, UNUSED),
            padded_codes(grid_places(range(5), range(24)), 128, UNUSED),
            padded_codes(grid_places(range(7, 12), sides), 112, UNUSED),
            padded_codes(grid_places(range(5), sides), 112, UNUSED),
            padded_codes(grid_places(range(1, 6), coarse_sides), 112, UNUSED),
            padded_codes(grid_places(range(5), coarse_sides), 112, UNUSED),
        ]
    ):
        by_column[: len(values), at] = values
    return by_row, by_column


def norm_rows(values, gain):
    middle = jnp.mean(values, axis=-1, keepdims=True)
    centered = values - middle
    spread = jnp.mean(centered * centered, axis=-1, keepdims=True)
    return centered * lax.rsqrt(spread + 1e-05) * gain


def dot(a, b):
    return jnp.dot(a, b, preferred_element_type=F32)


def dot_nt(a, b):
    return lax.dot_general(a, b, (((1,), (1,)), ((), ())), preferred_element_type=F32)


def kernel(
    shifts,
    fine_scale,
    coarse_scale,
    hbm_tokens,
    w_fine_qkv,
    w_fine_out,
    w_merge,
    w_coarse_qkv,
    w_coarse_out,
    hbm_fine_table,
    hbm_coarse_table,
    hbm_bias_index,
    hbm_fine_gain,
    hbm_merge_gain,
    hbm_coarse_gain,
    hbm_by_row,
    hbm_by_column,
    out,
    fine_qkv,
    fine_out,
    merge,
    coarse_qkv,
    coarse_out,
    pool,
    to_right,
    to_left,
    to_below,
    to_above,
    to_below_c,
    to_above_c,
    query,
    key,
    value,
    mixed,
    fine_after,
    coarse_pool,
    bias,
    tokens,
    fine_table,
    coarse_table,
    bias_index,
    fine_gain,
    merge_gain,
    coarse_gain,
    by_row,
    by_column,
    tables,
    to_below_k,
    to_above_k,
    send_sem,
    recv_sem,
    local_sem,
):
    lat, lon = lax.axis_index("lat"), lax.axis_index("lon")
    core, z_lo = lat % 2, lat // 2
    x, z_hi, y = lon // 8, (lon // 4) % 2, lon % 4
    z = z_hi * 8 + z_lo

    def place(x, y, z, core):
        x, y, z = (x + 4) % 4, (y + 4) % 4, (z + 16) % 16
        return ((z % 8) * 2 + core, x * 8 + (z // 8) * 4 + y)

    def along_z(d):
        return place(x, y, z + d, core)

    def along_x(d):
        return place(x + d, y, z, core)

    def along_y(d):
        return place(x, y + d, z, core)

    line = z * 2 + core

    def along_lat(d):
        spot = (line + d + 32) % 32
        return place(x, y, spot // 2, spot % 2)

    def along_lon(d):
        return (lat, (lon + d + 32) % 32)

    sibling = place(x, y, z, 1 - core)
    opposite = 4 - 8 * core
    hops = (opposite, 3, -3, 2, -2, 1, -1)

    barrier = pltpu.get_barrier_semaphore()
    senders = [along_z(-d) for d in hops]
    senders += [along_x(d) for d in (1, -1, 2)] + [along_y(d) for d in (1, -1, 2)]
    senders += [sibling, along_lon(1), along_lon(-1), along_lat(1), along_lat(-1)]
    for device in senders:
        pl.semaphore_signal(barrier, inc=1, device_id=device, device_id_type=MESH)

    local_count = [0]

    def bring(source, target):
        at = local_count[0]
        local_count[0] += 1
        copy = pltpu.make_async_copy(source, target, local_sem.at[at])
        copy.start()
        return copy

    first = [
        bring(hbm_tokens, tokens),
        bring(hbm_by_row, by_row),
        bring(hbm_by_column, by_column),
    ]
    later = [
        bring(hbm_fine_table, fine_table),
        bring(hbm_coarse_table, coarse_table),
        bring(hbm_bias_index, bias_index),
        bring(hbm_fine_gain, fine_gain),
        bring(hbm_merge_gain, merge_gain),
        bring(hbm_coarse_gain, coarse_gain),
    ]

    def picked(column, rows, row_at, first, width, offset=0):
        left = by_column[0:rows, column : column + 1] + offset
        right = by_row[row_at : row_at + 1, first : first + width]
        return jnp.where(left == right, 1.0, 0.0).astype(BF)

    counter = [0]
    sent = []

    def send(source, target, device):
        at = counter[0]
        counter[0] += 1
        copy = pltpu.make_async_remote_copy(
            src_ref=source,
            dst_ref=target,
            send_sem=send_sem.at[at],
            recv_sem=recv_sem.at[at],
            device_id=device,
            device_id_type=MESH,
        )
        copy.start()
        sent.append(copy)
        return copy

    def arrived(copies):
        for copy in copies:
            copy.wait_recv()

    class Gather:
        def __init__(self, shard, whole, halves):
            self.shard, self.whole, self.halves = shard, whole, halves

        def start(self):
            self.ready, self.waits = [], []
            for axis, part, pair_axis, small in self.halves:
                rows, columns = small
                source = self.shard.at[rows, columns]
                target = self.whole.at[z_lo, core, rows, columns]
                self.ready.append(bring(source, target))
                for d in hops:
                    self.waits.append(send(source, target, along_z(d)))

        def begun(self):
            for copy in self.ready:
                copy.wait()
            arrived(self.waits)
            self.ready, self.waits = [], []

        def pair(self):
            self.begun()
            for axis, part, pair_axis, (rows, columns) in self.halves:
                area = self.whole.at[:, core, rows, columns]
                self.waits.append(send(area, area, pair_axis(1)))

        def spread(self):
            self.begun()
            for axis, (rows, columns), pair_axis, small in self.halves:
                area = self.whole.at[:, core, rows, columns]
                for d in (1, -1, 2):
                    self.waits.append(send(area, area, axis(d)))

        def share(self):
            arrived(self.waits)
            part = self.whole.at[:, core]
            self.waits = [send(part, part, sibling)]

        def finish(self):
            arrived(self.waits)

    def by_x(part):
        return along_x, part(x), along_y, part(x, y % 2)

    def by_y(part):
        return along_y, part(y), along_x, part(y, x % 2)

    def corner(first, width):
        def part(g, half=None):
            rows = pl.ds(pl.multiple_of((g // 2) * 16, 16), 16)
            at, wide = first + (g % 2) * width, width
            if half is not None:
                at, wide = at + half * (width // 2), width // 2
            return rows, pl.ds(pl.multiple_of(at, 128), wide)

        return part

    def band(first, width):
        def part(g, half=None):
            if half is None:
                return pl.ds(pl.multiple_of(g * 32, 32), 32), pl.ds(first, width)
            return pl.ds(pl.multiple_of(g * 32 + half * 16, 16), 16), pl.ds(first, width)

        return part

    def quarters(axis, g, first):
        part = corner(first, 384)(g)
        return axis, part, None, part

    g_fine_qkv = Gather(
        w_fine_qkv, fine_qkv, [quarters(along_x, x, 0), quarters(along_y, y, 768)]
    )
    g_fine_out = Gather(w_fine_out, fine_out, [by_x(corner(0, 256))])
    g_merge = Gather(w_merge, merge, [by_x(band(0, 256)), by_y(band(256, 256))])
    g_coarse_qkv = Gather(w_coarse_qkv, coarse_qkv, [by_x(corner(0, 768))])
    g_coarse_out = Gather(w_coarse_out, coarse_out, [by_y(corner(0, 256))])

    pl.semaphore_wait(barrier, len(senders))
    g_fine_qkv.start()
    g_fine_out.start()
    g_merge.start()
    for copy in first:
        copy.wait()
    own = tokens[...]
    to_right[...] = dot(picked(5, 144, 0, OWN, 288), own).astype(BF)
    to_left[...] = dot(picked(6, 144, 0, OWN, 288), own).astype(BF)
    to_below[...] = dot(picked(7, 128, 0, OWN, 288), own).astype(BF)
    to_above[...] = dot(picked(8, 128, 0, OWN, 288), own).astype(BF)
    pool[OWN : OWN + 288, :] = own

    g_fine_qkv.spread()
    side_copies = [
        send(to_right, pool.at[pl.ds(LEFT, 144)], along_lon(1)),
        send(to_left, pool.at[pl.ds(RIGHT, 144)], along_lon(-1)),
    ]
    row_copies = [
        send(to_below, pool.at[pl.ds(ABOVE, 128)], along_lat(1)),
        send(to_above, pool.at[pl.ds(BELOW, 128)], along_lat(-1)),
    ]
    bias[...] = jnp.zeros((16, PAD, 128), F32)
    tables[...] = jnp.zeros((16, 256), F32)
    for copy in later:
        copy.wait()
    tables[0:HEADS, 0:253] = fine_table[...]
    tables[HEADS : 2 * HEADS, 0:253] = coarse_table[...]
    table = tables[...]
    top = table.astype(BF)
    rest = table - top.astype(F32)
    middle = rest.astype(BF)
    bottom = (rest - middle.astype(F32)).astype(BF)
    table_parts = jnp.concatenate([top, middle, bottom], axis=0)
    levels = lax.broadcasted_iota(jnp.int32, (256, WIN), 0)

    def bias_rows(group, carry):
        rows = bias_index[pl.ds(pl.multiple_of(group * 8, 8), 8), :]
        for i in range(8):
            hot = jnp.where(levels == rows[i : i + 1, :], 1.0, 0.0).astype(BF)
            parts = dot(table_parts, hot)
            looked = (parts[0:16] + parts[16:32] + parts[32:48]) * LOG2E
            bias[:, pl.ds(group * 8 + i, 1), 0:WIN] = looked.reshape(16, 1, WIN)
        return carry

    lax.fori_loop(0, WIN // 8, bias_rows, 0)

    g_fine_qkv.share()
    g_fine_out.pair()
    g_merge.pair()

    lane = lax.broadcasted_iota(jnp.int32, (1, 128), 1)
    low = jnp.where(lane < 64, 1.0, 0.0).astype(BF)
    high = jnp.where(lane < 64, 0.0, 1.0).astype(BF)
    position = lax.broadcasted_iota(jnp.int32, (PAD, 128), 0)
    row_of = jnp.zeros((PAD, 128), jnp.int32)
    for r in range(1, WLAT):
        row_of = row_of + jnp.where(position >= WLON * r, 1, 0)
    ones_row = lax.broadcasted_iota(jnp.int32, (256, 256), 0) // 64
    ones_column = lax.broadcasted_iota(jnp.int32, (256, 256), 1) // 64
    same_head = jnp.where(ones_row == ones_column, 1.0, 0.0).astype(BF)

    def scale_row(scale):
        head_of = lax.broadcasted_iota(jnp.int32, (1, D), 1) // 64
        row = jnp.zeros((1, D), F32)
        for n in range(HEADS):
            row = jnp.where(head_of == n, scale[n] * LOG2E, row)
        return row

    def framed(level, windows, column, row_at, cells, first, width):
        offset = shifts[level, 0] * 128 + shifts[level, 1]
        at, count = windows
        left = by_column[at * PAD : (at + count) * PAD, column : column + 1] + offset
        right = by_row[row_at : row_at + 1, first : first + width]
        hot = jnp.where(left == right, 1.0, 0.0).astype(BF)
        return dot(hot, cells[first : first + width, :])

    def project(windows, cells, weights, scale):
        scales = scale_row(scale)
        at, count = windows
        frame = cells.astype(BF)
        for n in range(6):
            block = weights[:, :, :, 256 * n : 256 * n + 256].reshape(D, 256)
            rounded = dot(frame, block).astype(BF)
            columns = slice(256 * (n % 2), 256 * (n % 2) + 256)
            if n < 4:
                full = rounded.astype(F32)
                square = dot((full * full).astype(BF), same_head)
                full = full * lax.rsqrt(square + 1e-06)
                if n < 2:
                    full = full * scales[:, columns]
                rounded = full.astype(BF)
            target = (query, key, value)[n // 2]
            target[at : at + count, :, columns] = rounded.reshape(count, PAD, 256)

    def attend(level, windows, row_block, rows_here):
        first_row = lat * rows_here + shifts[level, 0] - WLAT
        at, count = windows

        def one(w, carry):
            latitude = row_of + (first_row + WLAT * row_block(w))
            here = (latitude >= 0) & (latitude < rows_here * 16) & (position < WIN)
            keep = jnp.where(here, 1.0, 0.0).astype(BF)
            for p in range(HEADS // 2):
                columns = slice(128 * p, 128 * p + 128)
                q = query[at + w, :, columns]
                pair = jnp.concatenate([q * low, q * high], axis=0)
                scores = dot_nt(pair, key[at + w, :, columns])
                own_bias = bias[8 * level + 2 * p : 8 * level + 2 * p + 2, :, 0:PAD]
                powers = jnp.exp2(scores + own_bias.reshape(2 * PAD, PAD)).astype(BF)
                kept = jnp.concatenate([value[at + w, :, columns] * keep, keep], axis=1)
                both = dot(powers, kept)
                mine = jnp.where(lane < 64, both[0:PAD, 0:128], both[PAD : 2 * PAD, 0:128])
                total = jnp.where(lane < 64, both[0:PAD, 128:256], both[PAD : 2 * PAD, 128:256])
                taken = mine / total
                mixed[at + w, :, columns] = taken.astype(BF)
            return carry

        lax.fori_loop(0, count, one, 0, unroll=True)

    def finish(level, windows, column, rows, row_at, weights, base, gain):
        offset = shifts[level, 0] * 128 + shifts[level, 1]
        left = by_column[0:rows, column : column + 1] - offset
        right = by_row[row_at : row_at + 1, 0 : windows * PAD]
        hot = jnp.where(left == right, 1.0, 0.0).astype(BF)
        taken = dot(hot, mixed[0:windows].reshape(windows * PAD, D)).astype(BF)
        branch = dot(taken, weights[...].reshape(D, D))
        return (base + norm_rows(branch, gain)).astype(BF)

    g_fine_qkv.finish()
    g_fine_out.spread()
    g_merge.spread()
    arrived(row_copies)
    frame = framed(0, (0, 3), 0, 0, pool, ABOVE, 544)
    project((0, 3), frame, fine_qkv, fine_scale)
    attend(0, (0, 3), lambda w: w, 12)

    arrived(side_copies)
    near = pool[OWN : OWN + 576, :]
    to_below_c[...] = dot(picked(9, 112, 0, OWN, 576), near).astype(BF)
    to_above_c[...] = dot(picked(10, 112, 0, OWN, 576), near).astype(BF)
    row_copies = [
        send(to_below_c, pool.at[pl.ds(ABOVE_C, 112)], along_lat(1)),
        send(to_above_c, pool.at[pl.ds(BELOW_C, 112)], along_lat(-1)),
    ]
    g_coarse_qkv.start()
    g_coarse_out.start()
    frame = framed(0, (3, 2), 0, 0, pool, OWN, 576)
    project((3, 2), frame, fine_qkv, fine_scale)
    attend(0, (3, 2), lambda w: 1, 12)

    frame = framed(0, (5, 4), 0, 0, pool, 0, ABOVE_C)
    arrived(row_copies)
    frame = frame + framed(0, (5, 4), 0, 0, pool, ABOVE_C, POOL - ABOVE_C)
    g_fine_out.share()
    g_merge.share()
    project((5, 4), frame, fine_qkv, fine_scale)
    g_coarse_qkv.pair()
    g_coarse_out.pair()
    attend(0, (5, 4), lambda w: 2 * (w // 2), 12)
    g_fine_out.finish()
    in_quads = dot(picked(1, 320, 0, OWN, 288), tokens[...])
    fine_after[...] = finish(0, 9, 1, 320, 1, fine_out, in_quads, fine_gain[...])
    g_coarse_qkv.spread()
    g_coarse_out.spread()
    g_merge.finish()
    merged = jnp.zeros((PAD, D), F32)
    for p in range(4):
        rows = merge[2 * p : 2 * p + 2].reshape(D, D)
        merged = merged + dot(fine_after[PAD * p : PAD * p + PAD, :], rows)
    coarse_pool[0:PAD, :] = norm_rows(merged, merge_gain[...]).astype(BF)
    mine = coarse_pool.at[pl.ds(0, PAD)]
    side_copies = [
        send(mine, coarse_pool.at[pl.ds(C_LEFT, PAD)], along_lon(1)),
        send(mine, coarse_pool.at[pl.ds(C_RIGHT, PAD)], along_lon(-1)),
    ]
    row_copies = [
        send(mine, coarse_pool.at[pl.ds(C_ABOVE, PAD)], along_lat(1)),
        send(mine, coarse_pool.at[pl.ds(C_BELOW, PAD)], along_lat(-1)),
    ]
    arrived(side_copies)
    near = coarse_pool[0 : 3 * PAD, :]
    to_below_k[...] = dot(picked(11, 112, 3, 0, 3 * PAD), near).astype(BF)
    to_above_k[...] = dot(picked(12, 112, 3, 0, 3 * PAD), near).astype(BF)
    row_copies += [
        send(to_below_k, coarse_pool.at[pl.ds(C_ABOVE_C, 112)], along_lat(1)),
        send(to_above_k, coarse_pool.at[pl.ds(C_BELOW_C, 112)], along_lat(-1)),
    ]
    g_coarse_qkv.share()
    g_coarse_out.share()
    frame = framed(1, (0, 4), 2, 3, coarse_pool, 0, C_ABOVE)
    g_coarse_qkv.finish()
    arrived(row_copies[:2])
    frame = frame + framed(1, (0, 4), 2, 3, coarse_pool, C_ABOVE, C_ABOVE_C - C_ABOVE)
    arrived(row_copies[2:])
    corners = CPOOL - C_ABOVE_C
    frame = frame + framed(1, (0, 4), 2, 3, coarse_pool, C_ABOVE_C, corners)
    project((0, 4), frame, coarse_qkv, coarse_scale)
    attend(1, (0, 4), lambda w: w // 2, 6)
    g_coarse_out.finish()
    base = coarse_pool[0:PAD, :].astype(F32)
    coarse_after = finish(1, 4, 3, PAD, 4, coarse_out, base, coarse_gain[...]).astype(F32)
    for p in range(4):
        part = fine_after[PAD * p : PAD * p + PAD, :].astype(F32) + coarse_after
        fine_after[PAD * p : PAD * p + PAD, :] = part.astype(BF)
    out[...] = dot(picked(4, 288, 2, 0, 320), fine_after[...]).astype(BF)
    for copy in sent:
        copy.wait_send()


COPIES = 12 + 21 + 12 + 23 + 12 + 12


def per_device(
    tokens,
    fine_qkv,
    fine_out,
    fine_scale,
    fine_table,
    fine_gain,
    merge_weight,
    merge_gain,
    coarse_qkv,
    coarse_out,
    coarse_scale,
    coarse_table,
    coarse_gain,
    shifts,
    bias_index,
):
    by_row, by_column = code_tables()
    rows, columns, width = tokens.shape
    smem = pl.BlockSpec(memory_space=pltpu.SMEM)
    vmem = pl.BlockSpec(memory_space=pltpu.VMEM)
    hbm = pl.BlockSpec(memory_space=pltpu.HBM)
    result = pl.pallas_call(
        kernel,
        out_shape=jax.ShapeDtypeStruct((rows * columns, width), BF),
        in_specs=[smem] * 3 + [hbm] * 14,
        out_specs=vmem,
        scratch_shapes=[
            pltpu.VMEM((8, 2, 32, 1536), BF),
            pltpu.VMEM((8, 2, 32, 512), BF),
            pltpu.VMEM((8, 2, 128, 512), BF),
            pltpu.VMEM((8, 2, 32, 1536), BF),
            pltpu.VMEM((8, 2, 32, 512), BF),
            pltpu.VMEM((POOL, D), BF),
            pltpu.VMEM((144, D), BF),
            pltpu.VMEM((144, D), BF),
            pltpu.VMEM((128, D), BF),
            pltpu.VMEM((128, D), BF),
            pltpu.VMEM((112, D), BF),
            pltpu.VMEM((112, D), BF),
            pltpu.VMEM((9, PAD, D), BF),
            pltpu.VMEM((9, PAD, D), BF),
            pltpu.VMEM((9, PAD, D), BF),
            pltpu.VMEM((9, PAD, D), BF),
            pltpu.VMEM((320, D), BF),
            pltpu.VMEM((CPOOL, D), BF),
            pltpu.VMEM((16, PAD, 128), F32),
            pltpu.VMEM((288, D), BF),
            pltpu.VMEM((HEADS, 253), F32),
            pltpu.VMEM((HEADS, 253), F32),
            pltpu.VMEM((WIN, WIN), jnp.int32),
            pltpu.VMEM((1, D), F32),
            pltpu.VMEM((1, D), F32),
            pltpu.VMEM((1, D), F32),
            pltpu.VMEM((8, 1152), jnp.int32),
            pltpu.VMEM((720, 128), jnp.int32),
            pltpu.VMEM((16, 256), F32),
            pltpu.VMEM((112, D), BF),
            pltpu.VMEM((112, D), BF),
            pltpu.SemaphoreType.DMA((COPIES,)),
            pltpu.SemaphoreType.DMA((COPIES,)),
            pltpu.SemaphoreType.DMA((20,)),
        ],
        compiler_params=pltpu.CompilerParams(
            collective_id=0, has_side_effects=True, vmem_limit_bytes=64 << 20
        ),
    )(
        shifts,
        fine_scale,
        coarse_scale,
        tokens.reshape(rows * columns, width),
        fine_qkv,
        fine_out,
        merge_weight,
        coarse_qkv,
        coarse_out,
        fine_table.T,
        coarse_table.T,
        bias_index,
        fine_gain.reshape(1, -1),
        merge_gain.reshape(1, -1),
        coarse_gain.reshape(1, -1),
        jnp.asarray(by_row),
        jnp.asarray(by_column),
    )
    return result.reshape(rows, columns, width)


def solution(mesh):
    placed = (
        P("lat", "lon", None),
        P("lat", None),
        P("lat", None),
        P(),
        P(),
        P(),
        P("lat", None),
        P(),
        P("lat", None),
        P("lat", None),
        P(),
        P(),
        P(),
        P(),
        P(),
    )
    return jax.shard_map(
        per_device, mesh=mesh, in_specs=placed, out_specs=P("lat", "lon", None), check_vma=False
    )
```
